32 devices in a mesh: dom: 32 (over z, y, x, core).
Axes of the slice: x: 2, y: 2, z: 4, core: 2. Of those that a mesh axis runs over, the one named last changes fastest.
Arguments:
- adjoint_end: bfloat16 [256, 384, 256], P('dom'), may hold values from -6 to 6
- operator_blocks: bfloat16 [256, 6, 384, 384], P('dom'), may hold values from -0.125 to 0.125
- block_cols: int32 [256, 6], P('dom'), may hold values from -1 to 15, as said below
- halo_send: int32 [32, 4, 2], P('dom'), may hold values from -1 to 7, as said below
- wet_cells: int32 [256, 128], P('dom'), may hold values 0 or 1
- gauge_cells: int32 [256], replicated, may hold values from 0 to 32767
- window_first: int32 [256], replicated, may hold values from 0 to 1
- window_len: int32 [256], replicated, may hold values from 1 to 2
- gauge_gain: float32 [256], replicated, may hold values from 0.5 to 4
- snapshots: float32 [2, 256, 384], P(None, 'dom'), may hold values from -27 to 27, as said below
Outputs:
- adjoint_start: bfloat16 [256, 384, 256], P('dom')
- sensitivity: float32 [256, 128, 256], P('dom')
The draws below stay inside these ranges and needn't reach their ends.
Inputs may be any that keep to these rules, and one draw needn't show every extreme that they name: `block_cols`: in each row entry 0 is the row's own local block; live entries come first and -1 fills the rest; received slots named are only those whose sending device exists. `halo_send`: for each device and neighbour o the 2 blocks are distinct; -1 exactly where device d + off_o does not exist. `snapshots`: nonzero values.
All inputs are finite; a program needn't handle non-finite values. No bound on the sum of `wet_cells` on one device may be relied on, other than what follows from the above.
Results may differ from the reference program's by a relative error of at most 0.0013.
The reference program's roundings to bfloat16 on the way count: a program that leaves them out, or rounds other values in their place, can miss the bound.
Values may be sent and summed in bfloat16 or wider, within the bound.
No kernel may reach another device: no remote copies, remote signals or barrier semaphores. Data moves between devices by JAX's collectives and lax.ppermute only.
A program may use at most 128 MiB of HBM per device.

```python
import math
import jax
import jax.numpy as jnp
from jax import lax

BD = 8
CB = 128
NF = 256
KN = 6
CAP = 2
STEPS = 2
BLOCKS = 256
CELLS = 32768


neighbour_offsets = (-2, -1, 1, 2)


def topology(key):
    devices = BLOCKS // BD
    offsets = jnp.array(neighbour_offsets, jnp.int32)
    key_pick, key_heavy, key_own = jax.random.split(jax.random.fold_in(key, 7), 3)
    pick_keys = jax.random.split(key_pick, devices * 4)
    picks = jax.vmap(lambda single: jax.random.permutation(single, BD)[:CAP])(pick_keys).reshape(devices, 4, CAP)
    device_ids = jnp.arange(devices, dtype=jnp.int32)[:, None]
    target = device_ids + offsets[None, :]
    exists = (target >= 0) & (target < devices)
    sends = jnp.where(exists[:, :, None], picks, -1).astype(jnp.int32)
    source = device_ids - offsets[None, :]
    arrives = (source >= 0) & (source < devices)
    heavy = jax.random.randint(key_heavy, (devices,), 0, 4) == 0
    heavy = heavy.at[0].set(False).at[1].set(True)
    lighter = min(KN, 1 + (4 * CAP + BD - 1) // BD)
    live = jnp.where(heavy, KN, lighter).astype(jnp.int32)[:, None, None]
    row_ids = jnp.arange(BD, dtype=jnp.int32)[None, :, None]
    entry = jnp.arange(KN, dtype=jnp.int32)[None, None, :]
    position = row_ids * (live - 1) + entry - 1
    slot_group = jnp.clip(position // CAP, 0, 3)
    group_ids = jnp.arange(4, dtype=jnp.int32)
    arrived = jnp.any((slot_group[:, :, :, None] == group_ids) & arrives[:, None, None, :], axis=-1)
    use_halo = (entry >= 1) & (position >= 0) & (position < 4 * CAP) & arrived
    own_pick = jax.random.randint(key_own, (devices, BD, KN), 0, BD)
    columns = jnp.where(entry == 0, row_ids, jnp.where(use_halo, BD + position, own_pick))
    columns = jnp.where(entry < live, columns, -1).astype(jnp.int32)
    return (columns.reshape(devices * BD, KN), sends)


def draw_block_cols(key, part):
    return topology(key)[0]


def draw_halo_send(key, part):
    return topology(key)[1]


def draw_snapshots(key, part):
    key_mag, key_sign = jax.random.split(jax.random.fold_in(key, 11), 2)
    shape = (STEPS, BLOCKS, 3 * CB)
    along = jnp.arange(BLOCKS, dtype=jnp.float32)[None, :, None] / (BLOCKS - 1)
    signs = jnp.where(jax.random.bernoulli(key_sign, 0.5, shape), 1.0, -1.0)
    rise = 1.0 + 2.0 * along
    magnitude = jnp.exp(jax.random.uniform(key_mag, shape, jnp.float32, jnp.log(0.3), jnp.log(3.0)))
    return (signs * magnitude * rise).astype(jnp.float32)


def set_ends(values, stream_key, least, top_value):
    index_at = [jax.random.randint(jax.random.fold_in(stream_key, axis), (), 0, length) for axis, length in enumerate(values.shape)]
    longest = values.shape.index(max(values.shape))
    beside = index_at[:longest] + [(index_at[longest] + 1) % values.shape[longest]] + index_at[longest + 1:]
    return values.at[tuple(index_at)].set(least).at[tuple(beside)].set(top_value)


def block_levels(own_key, shape, shards, smallest, top_value):
    def one(axis_at, parts):
        draws = jax.random.uniform(jax.random.fold_in(jax.random.fold_in(own_key, 6), axis_at), (parts,), jnp.float32, smallest / len(shards), top_value / len(shards))
        return jnp.repeat(jnp.exp(draws), shape[axis_at] // parts).reshape((-1,) + (1,) * (len(shape) - axis_at - 1))

    level = one(*shards[0])
    for cut in shards[1:]:
        level = level * one(*cut)
    return level


def noise(own_key, dims, scale, most, cuts=(), kind=jnp.bfloat16):
    gain = block_levels(own_key, dims, cuts, -0.22, 0.18) if cuts else 1.0
    drawn = jax.random.normal(own_key, dims, jnp.float32) * scale * gain
    return jnp.minimum(jnp.maximum(drawn, -most), most).astype(kind)


def setup_inputs(seed: int = 0) -> dict:
    splits = jax.random.split(jax.random.key(seed), 11)
    adjoint_end = noise(splits[0], (BLOCKS, 3 * CB, NF), 1.0, 6.0, ((0, 32),))
    operator_blocks = noise(splits[1], (BLOCKS, KN, 3 * CB, 3 * CB), (3 * CB * KN) ** -0.5, 0.125, ((0, 32),))
    block_cols = draw_block_cols(jax.random.fold_in(splits[10], 71), 0)
    halo_send = draw_halo_send(jax.random.fold_in(splits[10], 71), 0)
    wet_cells = set_ends((jax.random.randint(splits[4], (BLOCKS, CB), 0, 4) < 3).astype(jnp.int32), jax.random.fold_in(splits[4], 1), 0, 1)
    gauge_cells = set_ends(jax.random.randint(splits[5], (NF,), 0, CELLS), jax.random.fold_in(splits[5], 1), 0, CELLS - 1).astype(jnp.int32)
    window_first = set_ends(jax.random.randint(splits[6], (NF,), 0, STEPS), jax.random.fold_in(splits[6], 1), 0, STEPS - 1).astype(jnp.int32)
    window_len = set_ends(jax.random.randint(splits[7], (NF,), 1, STEPS + 1), jax.random.fold_in(splits[7], 1), 1, STEPS).astype(jnp.int32)
    gauge_gain = jnp.clip(jnp.exp(jax.random.uniform(splits[8], (NF,), jnp.float32, math.log(0.5), math.log(4.0))), 0.5, 4.0)
    snapshots = draw_snapshots(jax.random.fold_in(splits[10], 71), 0)
    return {"adjoint_end": adjoint_end, "operator_blocks": operator_blocks, "block_cols": block_cols, "halo_send": halo_send, "wet_cells": wet_cells, "gauge_cells": gauge_cells, "window_first": window_first, "window_len": window_len, "gauge_gain": gauge_gain, "snapshots": snapshots}


neighbour_offsets = (-2, -1, 1, 2)

def global_columns(block_cols, halo_send):
    devices = BLOCKS // BD
    offsets = jnp.array(neighbour_offsets, jnp.int32)
    row_device = (jnp.arange(BLOCKS, dtype=jnp.int32) // BD)[:, None]
    own_block = row_device * BD + jnp.clip(block_cols, 0, BD - 1)
    slot_number = jnp.clip(block_cols - BD, 0, 4 * CAP - 1)
    group = slot_number // CAP
    within = slot_number % CAP
    sender = jnp.clip(row_device - offsets[group], 0, devices - 1)
    sent_block = halo_send[sender, group, within]
    remote_block = sender * BD + jnp.clip(sent_block, 0, BD - 1)
    glob = jnp.where(block_cols < BD, own_block, remote_block).astype(jnp.int32)
    return (glob, block_cols >= 0)

def reference(adjoint_end, operator_blocks, block_cols, halo_send, wet_cells, gauge_cells, window_first, window_len, gauge_gain, snapshots):
    glob, valid = global_columns(block_cols, halo_send)
    cell_ids = jnp.arange(CELLS, dtype=jnp.int32).reshape(BLOCKS, CB)
    gauge_hit = (cell_ids[:, :, None] == gauge_cells[None, None, :]).astype(jnp.float32)
    wet_rows = jnp.tile(wet_cells.astype(jnp.float32), (1, 3))[:, :, None]
    adjoint = adjoint_end
    raw = jnp.zeros((BLOCKS, CB, NF), jnp.float32)
    for step_index in range(STEPS):
        current = adjoint

        def one_row(items):
            columns, usable, weights = items
            picked = current[columns].astype(jnp.float32)
            picked = jnp.where(usable[:, None, None], picked, jnp.zeros((), jnp.float32))
            return jnp.einsum('kij,kjf->if', weights.astype(jnp.float32), picked)
        coupled = lax.map(one_row, (glob, valid, operator_blocks))
        active = ((window_first <= step_index) & (step_index < window_first + window_len)).astype(jnp.float32) * gauge_gain
        source = gauge_hit * active[None, None, :]
        source_full = jnp.concatenate([source, jnp.zeros((BLOCKS, 2 * CB, NF), jnp.float32)], axis=1)
        updated = wet_rows * (current.astype(jnp.float32) + coupled) + source_full
        adjoint = updated.astype(jnp.bfloat16)
        saved = snapshots[step_index].reshape(BLOCKS, 3, CB)[:, :, :, None]
        raw = raw + lax.optimization_barrier(jnp.sum(saved * adjoint.astype(jnp.float32).reshape(BLOCKS, 3, CB, NF), axis=1))
    meansq = lax.optimization_barrier(jnp.sum(raw * raw, axis=(0, 1))) / CELLS
    sensitivity = raw * lax.rsqrt(meansq + 1e-06)[None, None, :]
    return (adjoint, sensitivity)
```

```python
import functools

import jax
import jax.numpy as jnp
from jax import lax
from jax.experimental import pallas as pl
from jax.experimental.pallas import tpu as pltpu
from jax.sharding import PartitionSpec as P

ROUTES = ("swap", "cross", "inner", "outer")


def route_pairs(devices):
    swap = [(i, i ^ 1) for i in range(devices)]
    cross = [(i, i + 1) for i in range(1, devices - 1, 2)]
    inner = [(i, i ^ 2) for i in range(devices)]
    outer = [(i, i + 2) for i in range(devices - 2) if i & 2]
    both = lambda pairs: pairs + [(j, i) for i, j in pairs]
    return dict(swap=swap, cross=both(cross), inner=inner, outer=both(outer))


def send_groups(device):
    core, chip = device % 2, (device // 2) % 2
    return dict(swap=2 - core, cross=1 + core, inner=3 - 3 * chip, outer=3 * chip)


def receive_groups(device):
    core, chip = device % 2, (device // 2) % 2
    return dict(swap=1 + core, cross=2 - core, inner=3 * chip, outer=3 - 3 * chip)


def exchange(sends):
    pairs = route_pairs(lax.axis_size("dom"))
    return {r: lax.ppermute(sends[r], "dom", pairs[r]) for r in ("inner", "cross", "outer", "swap")}


def pick_kernel(halo, lam, *rest):
    outs, sems = dict(zip(ROUTES, rest[:4])), rest[4]
    groups = send_groups(lax.axis_index("dom"))
    copies = []
    for i, r in enumerate(ROUTES):
        for c in range(2):
            row = jnp.maximum(halo[groups[r], c], 0)
            copies.append(pltpu.make_async_copy(lam.at[row], outs[r].at[c], sems.at[i, c]))
    for copy in copies:
        copy.start()
    for copy in copies:
        copy.wait()


def pick_sends(halo, lam):
    part = jax.ShapeDtypeStruct((2,) + lam.shape[1:], lam.dtype)
    outs = pl.pallas_call(
        pick_kernel,
        name="pick_sends",
        out_shape=[part] * 4,
        in_specs=[pl.BlockSpec(memory_space=pltpu.SMEM), pl.BlockSpec(memory_space=pl.ANY)],
        out_specs=[pl.BlockSpec(memory_space=pl.ANY)] * 4,
        scratch_shapes=[pltpu.SemaphoreType.DMA((4, 2))],
    )(halo, lam)
    return dict(zip(ROUTES, outs))


def step_kernel(late, last, step, devices, *refs):
    refs = list(refs)
    take = lambda n: [refs.pop(0) for _ in range(n)]
    cols, halo, lam, ops, aux, gauges = take(6)
    received = take(4) if late else []
    (done,) = take(1) if late else (None,)
    done_raw, done_squares = take(2) if late and last else (None, None)
    (new,) = take(1)
    raw, squares = take(2) if last else (None, None)
    sends = dict(zip(ROUTES, take(4))) if late and not last else {}
    ext, opbuf, out, rawbuf, ext_sem, op_sem, out_sem, raw_sem, send_sem, flags = refs

    owned, entries = ops.shape[0], ops.shape[1]
    rows, width = lam.shape[1], lam.shape[2]
    cells = rows // 3
    zero_block = ext.shape[0] - 1
    position = lax.axis_index("dom")

    def pairs_of(b):
        live = 0
        for k in range(entries):
            live = live + (cols[b, k] >= 0).astype(jnp.int32)
        return (live + 1) // 2

    def is_mine(b):
        top = cols[b, 0]
        for k in range(1, entries):
            top = jnp.maximum(top, cols[b, k])
        return (top >= owned) if late else (top < owned)

    copies = [pltpu.make_async_copy(lam, ext.at[pl.ds(0, owned)], ext_sem.at[4])]
    if late:
        groups = receive_groups(position)
        for i, r in enumerate(ROUTES):
            copies.append(
                pltpu.make_async_copy(received[i], ext.at[pl.ds(owned + 2 * groups[r], 2)], ext_sem.at[i])
            )

    def op_copy(b, p):
        return pltpu.make_async_copy(
            ops.at[b, pl.ds(2 * p, 2)], opbuf.at[b, pl.ds(2 * p, 2)], op_sem.at[b, p]
        )

    for copy in copies:
        copy.start()

    @pl.loop(0, owned)
    def _(b):
        mine = is_mine(b)
        number = pairs_of(b)
        flags[b] = jnp.where(mine, number, 0)
        for p in range(entries // 2):

            @pl.when(jnp.logical_and(mine, number > p))
            def _():
                op_copy(b, p).start()

    send_rows = []
    if sends:
        groups = send_groups(position)
        for i, r in enumerate(ROUTES):
            for c in range(2):
                send_rows.append((i, r, c, jnp.maximum(halo[groups[r], c], 0)))
        for i, r, c, row in send_rows:

            @pl.when(flags[row] == 0)
            def _(i=i, r=r, c=c, row=row):
                pltpu.make_async_copy(done.at[row], sends[r].at[c], send_sem.at[i, c]).start()

    ext[zero_block] = jnp.zeros((rows, width), ext.dtype)
    if last:
        if late:
            squares[...] = jnp.broadcast_to(done_squares[...], squares.shape)
        else:
            squares[...] = jnp.zeros(squares.shape, jnp.float32)
    for copy in copies:
        copy.wait()

    first = gauges[1:2, :]
    active = jnp.where(
        jnp.logical_and(first <= step, step < first + gauges[2:3, :]), gauges[3:4, :], 0.0
    )
    own_cells = lax.broadcasted_iota(jnp.int32, (cells, width), 0)

    def finish(b, total):
        wet = aux[b, :, 0:1]
        where = gauges[0:1, :].astype(jnp.int32) - (position * owned + b) * cells
        source = jnp.where(own_cells == where, active, 0.0)
        gathered = None
        for c in range(3):
            part = pl.ds(c * cells, cells)
            before = ext[b, part, :].astype(jnp.float32)
            updated = wet * (before + total[c * cells : (c + 1) * cells])
            if c == 0:
                updated = updated + source
            updated = updated.astype(jnp.bfloat16)
            out[b, part, :] = updated
            if last:
                term = aux[b, :, 1 + c : 2 + c] * before
                gathered = term if gathered is None else gathered + term
                gathered = gathered + aux[b, :, 4 + c : 5 + c] * updated.astype(jnp.float32)
        if last:
            rawbuf[b] = gathered
            squares[...] += jnp.broadcast_to(
                jnp.sum(gathered * gathered, axis=0, keepdims=True), squares.shape
            )

    @pl.loop(0, owned)
    def _(b):
        number = flags[b]

        for n in range(1, entries // 2 + 1):

            @pl.when(number == n)
            def _(n=n):
                for p in range(n):
                    op_copy(b, p).wait()
                picked = []
                for k in range(2 * n):
                    col = cols[b, k]
                    picked.append(ext[jnp.where(col < 0, zero_block, col)])
                weights = jnp.concatenate([opbuf[b, k] for k in range(2 * n)], axis=1)
                total = jnp.dot(
                    weights, jnp.concatenate(picked, axis=0), preferred_element_type=jnp.float32
                )
                finish(b, total)

        @pl.when(number > 0)
        def _():
            pltpu.make_async_copy(out.at[b], new.at[b], out_sem.at[b]).start()
            if last:
                pltpu.make_async_copy(rawbuf.at[b], raw.at[b], raw_sem.at[b]).start()
            for i, r, c, row in send_rows:

                @pl.when(row == b)
                def _(i=i, r=r, c=c):
                    pltpu.make_async_copy(out.at[b], sends[r].at[c], send_sem.at[i, c]).start()

    @pl.loop(0, owned)
    def _(b):
        @pl.when(flags[b] > 0)
        def _():
            pltpu.make_async_copy(out.at[b], new.at[b], out_sem.at[b]).wait()
            if last:
                pltpu.make_async_copy(rawbuf.at[b], raw.at[b], raw_sem.at[b]).wait()

    for i, r, c, row in send_rows:
        pltpu.make_async_copy(out.at[0], sends[r].at[c], send_sem.at[i, c]).wait()


def step_rows(late, last, step, cols, halo, lam, ops, aux, gauges, received=None, early=None):
    owned, rows, width = lam.shape
    cells = rows // 3
    devices = lax.axis_size("dom")
    smem, vmem, hbm = (pl.BlockSpec(memory_space=m) for m in (pltpu.SMEM, pltpu.VMEM, pl.ANY))
    args = [cols, halo, lam, ops, aux, gauges]
    in_specs = [smem, smem, hbm, hbm, vmem, vmem]
    aliases = {}
    if late:
        args += [received[r] for r in ROUTES]
        in_specs += [hbm] * 4
        aliases[len(args)] = 0
        args.append(early[0])
        in_specs.append(hbm)
        if last:
            aliases[len(args)] = 1
            args += [early[1], early[2]]
            in_specs += [hbm, vmem]
    out_shape = [jax.ShapeDtypeStruct(lam.shape, lam.dtype)]
    out_specs = [hbm]
    if last:
        out_shape += [
            jax.ShapeDtypeStruct((owned, cells, width), jnp.float32),
            jax.ShapeDtypeStruct((devices if late else 1, width), jnp.float32),
        ]
        out_specs += [hbm, vmem]
    elif late:
        out_shape += [jax.ShapeDtypeStruct((2, rows, width), lam.dtype)] * 4
        out_specs += [hbm] * 4
    dma = pltpu.SemaphoreType.DMA
    return pl.pallas_call(
        functools.partial(step_kernel, late, last, step, devices),
        name=("late" if late else "early") + "_rows",
        out_shape=out_shape,
        in_specs=in_specs,
        out_specs=out_specs,
        input_output_aliases=aliases,
        scratch_shapes=[
            pltpu.VMEM((2 * owned + 1, rows, width), lam.dtype),
            pltpu.VMEM(ops.shape, ops.dtype),
            pltpu.VMEM(lam.shape, lam.dtype),
            pltpu.VMEM((owned, cells, width), jnp.float32),
            dma((5,)),
            dma((owned, ops.shape[1] // 2)),
            dma((owned,)),
            dma((owned,)),
            dma((4, 2)),
            pltpu.SMEM((owned,), jnp.int32),
        ],
        compiler_params=pltpu.CompilerParams(vmem_limit_bytes=40 * 1024 * 1024),
        cost_estimate=pl.CostEstimate(
            flops=2 * owned * 2 * rows * rows * width, bytes_accessed=8 << 20, transcendentals=0
        ),
    )(*args)


def scale_kernel(cells_total, sums, raw, out):
    meansq = jnp.sum(sums[...], axis=0, keepdims=True) / cells_total
    out[...] = raw[...] * lax.rsqrt(meansq + 1e-06)[None]


def scaled(sums, raw, cells_total):
    owned, cells, width = raw.shape
    return pl.pallas_call(
        functools.partial(scale_kernel, cells_total),
        name="scale",
        grid=(owned // 2,),
        out_shape=jax.ShapeDtypeStruct(raw.shape, raw.dtype),
        in_specs=[
            pl.BlockSpec(sums.shape, lambda i: (0, 0)),
            pl.BlockSpec((2, cells, width), lambda i: (i, 0, 0)),
        ],
        out_specs=pl.BlockSpec((2, cells, width), lambda i: (i, 0, 0)),
    )(sums, raw)


def per_device(
    adjoint_end,
    operator_blocks,
    block_cols,
    halo_send,
    wet_cells,
    gauge_cells,
    window_first,
    window_len,
    gauge_gain,
    snapshots,
):
    owned, cells = wet_cells.shape
    steps = snapshots.shape[0]
    devices = lax.axis_size("dom")
    halo = halo_send[0]
    factors = jnp.concatenate(
        [wet_cells.astype(jnp.float32)[:, None]]
        + [snapshots[t].reshape(owned, 3, cells) for t in range(steps)]
        + [jnp.zeros((owned, 1, cells), jnp.float32)],
        axis=1,
    )
    aux = jnp.swapaxes(factors, 1, 2)
    gauges = jnp.stack(
        [v.astype(jnp.float32) for v in (gauge_cells, window_first, window_len, gauge_gain)]
    )
    lam = adjoint_end
    sends = pick_sends(halo, lam)
    for step in range(steps):
        last = step == steps - 1
        common = (step, block_cols, halo, lam, operator_blocks, aux, gauges)
        received = exchange(sends)
        early = step_rows(False, last, *common)
        late = step_rows(True, last, *common, received=received, early=early)
        lam = late[0]
        if not last:
            sends = dict(zip(ROUTES, late[1:]))
    raw, squares = late[1:]
    sums = lax.all_to_all(squares, "dom", 0, 0, tiled=True)
    return (lam, scaled(sums, raw, devices * owned * cells))


def solution(mesh):
    return jax.shard_map(
        per_device,
        mesh=mesh,
        in_specs=(
            P("dom", None, None),
            P("dom", None, None, None),
            P("dom", None),
            P("dom", None, None),
            P("dom", None),
            P(),
            P(),
            P(),
            P(),
            P(None, "dom", None),
        ),
        out_specs=(P("dom", None, None), P("dom", None, None)),
        check_vma=False,
    )
```

```python
import functools

import jax
import jax.numpy as jnp
from jax import lax
from jax.experimental import pallas as pl
from jax.experimental.pallas import tpu as pltpu
from jax.sharding import PartitionSpec as P

ROUTES = ("swap", "cross", "inner", "outer")


def route_pairs(devices):
    swap = [(i, i ^ 1) for i in range(devices)]
    cross = [(i, i + 1) for i in range(1, devices - 1, 2)]
    inner = [(i, i ^ 2) for i in range(devices)]
    outer = [(i, i + 2) for i in range(devices - 2) if i & 2]
    both = lambda pairs: pairs + [(j, i) for i, j in pairs]
    return dict(swap=swap, cross=both(cross), inner=inner, outer=both(outer))


def send_groups(device):
    core, chip = device % 2, (device // 2) % 2
    return dict(swap=2 - core, cross=1 + core, inner=3 - 3 * chip, outer=3 * chip)


def receive_groups(device):
    core, chip = device % 2, (device // 2) % 2
    return dict(swap=1 + core, cross=2 - core, inner=3 * chip, outer=3 - 3 * chip)


def exchange(sends):
    pairs = route_pairs(lax.axis_size("dom"))
    return {r: lax.ppermute(sends[r], "dom", pairs[r]) for r in ("inner", "cross", "outer", "swap")}


def pinned(value):
    return pltpu.with_memory_space_constraint(value, pltpu.VMEM)


def pick_kernel(halo, lam, *rest):
    outs, sems = dict(zip(ROUTES, rest[:4])), rest[4]
    groups = send_groups(lax.axis_index("dom"))
    copies = []
    for i, r in enumerate(ROUTES):
        for c in range(2):
            row = jnp.maximum(halo[0, groups[r], c], 0)
            copies.append(pltpu.make_async_copy(lam.at[row], outs[r].at[c], sems.at[i, c]))
    for copy in copies:
        copy.start()
    for copy in copies:
        copy.wait()


def pick_sends(halo, lam):
    part = pltpu.VMEM((2,) + lam.shape[1:], lam.dtype)
    outs = pl.pallas_call(
        pick_kernel,
        name="pick_sends",
        out_shape=[part] * 4,
        in_specs=[pl.BlockSpec(memory_space=pltpu.SMEM), pl.BlockSpec(memory_space=pltpu.HBM)],
        out_specs=[pl.BlockSpec(memory_space=pltpu.VMEM)] * 4,
        scratch_shapes=[pltpu.SemaphoreType.DMA((4, 2))],
    )(halo, lam)
    return dict(zip(ROUTES, outs))


def step_kernel(late, last, step, *refs):
    refs = list(refs)
    take = lambda n: [refs.pop(0) for _ in range(n)]
    cols, halo, lam, ops, aux, gauges = take(6)
    received = take(4) if late else []
    take(1 + last if late else 0)
    done_squares = take(1)[0] if late and last else None
    (new,) = take(1)
    raw, squares = take(2) if last else (None, None)
    sends = dict(zip(ROUTES, take(4))) if late and not last else {}
    (slots,) = refs if late else (None,)

    owned, entries = ops.shape[0], ops.shape[1]
    rows, width = lam.shape[1], lam.shape[2]
    cells = rows // 3
    position = lax.axis_index("dom")

    if late:
        groups = receive_groups(position)
        for i, r in enumerate(ROUTES):
            slots[pl.ds(2 * groups[r], 2)] = received[i][...]
    if last:
        if late:
            squares[...] = jnp.broadcast_to(done_squares[...], squares.shape)
        else:
            squares[...] = jnp.zeros(squares.shape, jnp.float32)

    first = gauges[1:2, :]
    active = jnp.where(
        jnp.logical_and(first <= step, step < first + gauges[2:3, :]), gauges[3:4, :], 0.0
    )
    own_cells = lax.broadcasted_iota(jnp.int32, (cells, width), 0)

    def finish(b, total):
        wet = aux[b, :, 0:1]
        where = gauges[0:1, :].astype(jnp.int32) - (position * owned + b) * cells
        source = jnp.where(own_cells == where, active, 0.0)
        gathered = None
        for c in range(3):
            part = pl.ds(c * cells, cells)
            before = lam[b, part, :].astype(jnp.float32)
            updated = wet * (before + total[c * cells : (c + 1) * cells])
            if c == 0:
                updated = updated + source
            updated = updated.astype(jnp.bfloat16)
            new[b, part, :] = updated
            if last:
                term = aux[b, :, 1 + c : 2 + c] * before
                gathered = term if gathered is None else gathered + term
                gathered = gathered + aux[b, :, 4 + c : 5 + c] * updated.astype(jnp.float32)
        if last:
            raw[b] = gathered
            squares[...] += jnp.broadcast_to(
                jnp.sum(gathered * gathered, axis=0, keepdims=True)[None], squares.shape
            )

    def picked(b, k):
        col = cols[b, k]
        block = lam[jnp.clip(col, 0, owned - 1)]
        if late:
            block = jnp.where(col < owned, block, slots[jnp.maximum(col - owned, 0)])
        return jnp.where(col >= 0, block, jnp.zeros_like(block))

    def make_row(b, n):
        state = [lam[b]] + [picked(b, k) for k in range(1, 2 * n)]
        weights = jnp.concatenate([ops[b, k] for k in range(2 * n)], axis=1)
        total = jnp.dot(
            weights, jnp.concatenate(state, axis=0), preferred_element_type=jnp.float32
        )
        finish(b, total)

    def shape_of(b):
        live, top = 0, -1
        for k in range(entries):
            live = live + (cols[b, k] >= 0).astype(jnp.int32)
            top = jnp.maximum(top, cols[b, k])
        return (live + 1) // 2, (top >= owned) if late else (top < owned)

    def each_row():
        @pl.loop(0, owned)
        def _(b):
            pairs, mine = shape_of(b)
            for n in range(1, entries // 2 + 1):

                @pl.when(jnp.logical_and(mine, pairs == n))
                def _(n=n):
                    make_row(b, n)

    if late:
        plain = True
        for b in range(owned):
            pairs, mine = shape_of(b)
            plain = jnp.logical_and(plain, jnp.logical_and(mine, pairs == 1))

        @pl.when(plain)
        def _():
            for b in range(owned):
                make_row(b, 1)

        @pl.when(jnp.logical_not(plain))
        def _():
            each_row()
    else:
        each_row()

    if sends:
        groups = send_groups(position)
        for r in ROUTES:
            for c in range(2):
                sends[r][c] = new[jnp.maximum(halo[0, groups[r], c], 0)]


def step_rows(late, last, step, cols, halo, lam, ops, aux, gauges, received=None, early=None):
    owned, rows, width = lam.shape
    cells = rows // 3
    devices = lax.axis_size("dom")
    smem, vmem = (pl.BlockSpec(memory_space=m) for m in (pltpu.SMEM, pltpu.VMEM))
    args = [cols, halo, pinned(lam), pinned(ops), aux, gauges]
    aliases = {}
    if late:
        args += [pinned(received[r]) for r in ROUTES]
        for i in range(1 + last):
            aliases[len(args)] = i
            args.append(pinned(early[i]))
        if last:
            args.append(early[2])
    out_shape = [pltpu.VMEM(lam.shape, lam.dtype)]
    if last:
        out_shape += [
            pltpu.VMEM((owned, cells, width), jnp.float32),
            pltpu.VMEM((devices if late else 1, 1, width), jnp.float32),
        ]
    elif late:
        out_shape += [pltpu.VMEM((2, rows, width), lam.dtype)] * 4
    return pl.pallas_call(
        functools.partial(step_kernel, late, last, step),
        name=("late" if late else "early") + "_rows",
        out_shape=out_shape,
        in_specs=[smem, smem] + [vmem] * (len(args) - 2),
        out_specs=[vmem] * len(out_shape),
        input_output_aliases=aliases,
        scratch_shapes=[pltpu.VMEM((owned, rows, width), lam.dtype)] if late else [],
        compiler_params=pltpu.CompilerParams(vmem_limit_bytes=16 * 1024 * 1024),
        cost_estimate=pl.CostEstimate(
            flops=2 * owned * 2 * rows * rows * width, bytes_accessed=8 << 20, transcendentals=0
        ),
    )(*args)


def scale_kernel(cells_total, sums, raw, out, scaled_rows, sems):
    factor = lax.rsqrt(jnp.sum(sums[...], axis=0) / cells_total + 1e-06)
    copies = []
    for b in range(raw.shape[0]):
        scaled_rows[b] = raw[b] * factor
        copies.append(pltpu.make_async_copy(scaled_rows.at[b], out.at[b], sems.at[b]))
        copies[b].start()
    for copy in copies:
        copy.wait()


def scaled(sums, raw, cells_total):
    vmem = pl.BlockSpec(memory_space=pltpu.VMEM)
    return pl.pallas_call(
        functools.partial(scale_kernel, cells_total),
        name="scale",
        out_shape=jax.ShapeDtypeStruct(raw.shape, raw.dtype),
        in_specs=[vmem, vmem],
        out_specs=pl.BlockSpec(memory_space=pltpu.HBM),
        scratch_shapes=[
            pltpu.VMEM(raw.shape, raw.dtype),
            pltpu.SemaphoreType.DMA((raw.shape[0],)),
        ],
    )(sums, pinned(raw))


def per_device(
    adjoint_end,
    operator_blocks,
    block_cols,
    halo_send,
    wet_cells,
    gauge_cells,
    window_first,
    window_len,
    gauge_gain,
    snapshots,
):
    owned, cells = wet_cells.shape
    steps = snapshots.shape[0]
    devices = lax.axis_size("dom")
    factors = jnp.concatenate(
        [wet_cells.astype(jnp.float32)[:, None]]
        + [snapshots[t].reshape(owned, 3, cells) for t in range(steps)]
        + [jnp.zeros((owned, 1, cells), jnp.float32)],
        axis=1,
    )
    aux = jnp.swapaxes(factors, 1, 2)
    gauges = jnp.stack(
        [v.astype(jnp.float32) for v in (gauge_cells, window_first, window_len, gauge_gain)]
    )
    lam = adjoint_end
    sends = pick_sends(halo_send, lam)
    for step in range(steps):
        last = step == steps - 1
        common = (step, block_cols, halo_send, lam, operator_blocks, aux, gauges)
        received = exchange(sends)
        early = step_rows(False, last, *common)
        late = step_rows(True, last, *common, received=received, early=early)
        lam = late[0]
        if not last:
            sends = dict(zip(ROUTES, late[1:]))
    raw, squares = late[1:]
    sums = lax.all_to_all(squares, "dom", 0, 0, tiled=True)
    return (lam, scaled(sums, raw, devices * owned * cells))


def solution(mesh):
    return jax.shard_map(
        per_device,
        mesh=mesh,
        in_specs=(
            P("dom", None, None),
            P("dom", None, None, None),
            P("dom", None),
            P("dom", None, None),
            P("dom", None),
            P(),
            P(),
            P(),
            P(),
            P(None, "dom", None),
        ),
        out_specs=(P("dom", None, None), P("dom", None, None)),
        check_vma=False,
    )
```

```python
import functools

import jax
import jax.numpy as jnp
from jax import lax
from jax.experimental import pallas as pl
from jax.experimental.pallas import tpu as pltpu
from jax.sharding import PartitionSpec as P

PARTS = 2
PICK_COST = (4 << 20, 96 << 20)
EARLY_COST = 4 << 20
LATE_COST = ((4 << 20, 4 << 20), (4 << 20, 4 << 20))
ROUTES = ("swap", "cross", "inner", "outer")


def route_pairs(devices):
    swap = [(i, i ^ 1) for i in range(devices)]
    cross = [(i, i + 1) for i in range(1, devices - 1, 2)]
    inner = [(i, i ^ 2) for i in range(devices)]
    outer = [(i, i + 2) for i in range(devices - 2) if i & 2]
    both = lambda pairs: pairs + [(j, i) for i, j in pairs]
    return dict(swap=swap, cross=both(cross), inner=inner, outer=both(outer))


def send_groups(device):
    core, chip = device % 2, (device // 2) % 2
    return dict(swap=2 - core, cross=1 + core, inner=3 - 3 * chip, outer=3 * chip)


def receive_groups(device):
    core, chip = device % 2, (device // 2) % 2
    return dict(swap=1 + core, cross=2 - core, inner=3 * chip, outer=3 - 3 * chip)


def exchange(sends):
    pairs = route_pairs(lax.axis_size("dom"))
    return {r: lax.ppermute(sends[r], "dom", pairs[r]) for r in ("inner", "cross", "outer", "swap")}


def pinned(value):
    return pltpu.with_memory_space_constraint(value, pltpu.VMEM)


def in_hbm(value):
    return pltpu.with_memory_space_constraint(value, pltpu.HBM)


def pick_kernel(part, halo, lam, *rest):
    outs, sems = dict(zip(ROUTES, rest[:4])), rest[4]
    groups = send_groups(lax.axis_index("dom"))
    copies = []
    for i, r in enumerate(ROUTES):
        for c in range(2):
            row = jnp.maximum(halo[0, c, groups[r]], 0)
            copies.append(
                pltpu.make_async_copy(lam.at[row, :, pl.ds(*part)], outs[r].at[c], sems.at[i, c])
            )
    for copy in copies:
        copy.start()
    for copy in copies:
        copy.wait()


def pick_sends(part, cost, halo, lam):
    sent = pltpu.VMEM((2, lam.shape[1], part[1]), lam.dtype)
    outs = pl.pallas_call(
        functools.partial(pick_kernel, part),
        name="pick_sends",
        out_shape=[sent] * 4,
        in_specs=[pl.BlockSpec(memory_space=pltpu.SMEM), pl.BlockSpec(memory_space=pltpu.HBM)],
        out_specs=[pl.BlockSpec(memory_space=pltpu.VMEM)] * 4,
        scratch_shapes=[pltpu.SemaphoreType.DMA((4, 2))],
        compiler_params=pltpu.CompilerParams(vmem_limit_bytes=4 * 1024 * 1024),
        cost_estimate=pl.CostEstimate(flops=0, bytes_accessed=cost, transcendentals=0),
    )(halo, lam)
    return dict(zip(ROUTES, outs))


def lay_out_facts(facts, aux, gauges):
    wet, snapshots = facts[:2]
    owned, cells = wet.shape
    for i, fact in enumerate(facts[2:]):
        gauges[i : i + 1, :] = fact[...].astype(jnp.float32)
    for b in range(owned):
        rows = [wet[b : b + 1, :].astype(jnp.float32)]
        for t in range(snapshots.shape[0]):
            for c in range(3):
                rows.append(snapshots[t, b : b + 1, c * cells : (c + 1) * cells])
        rows.append(jnp.zeros((1, cells), jnp.float32))
        aux[b] = jnp.concatenate(rows, axis=0).T


def step_kernel(late, last, step, part, final, *refs):
    refs = list(refs)
    take = lambda n: [refs.pop(0) for _ in range(n)]
    cols, halo, lam, ops = take(4)
    begin = not late and step == 0
    facts = take(6) if begin else None
    aux, gauges = (None, None) if begin else take(2)
    received = take(4) if late else []
    take(1 + last if late else 0)
    done_squares = take(1)[0] if late and last else None
    (new,) = take(1)
    raw, squares = take(2) if last else (None, None)
    sends = dict(zip(ROUTES, take(4))) if late and not last else {}
    if begin:
        aux, gauges, kept, op_sem = take(4)
        far, ops = ops, kept
    (slots,) = refs if late else (None,)

    owned, entries = ops.shape[0], ops.shape[1]
    rows, width = lam.shape[1], part[1]
    cells = rows // 3
    here = pl.ds(*part)
    position = lax.axis_index("dom")

    if late:
        groups = receive_groups(position)
        for i, r in enumerate(ROUTES):
            slots[pl.ds(2 * groups[r], 2)] = received[i][...]
    if last:
        if late:
            squares[...] = jnp.broadcast_to(done_squares[...], squares.shape)
        else:
            squares[...] = jnp.zeros(squares.shape, jnp.float32)

    def fetch(b, p):
        pair = pl.ds(2 * p, 2)
        return pltpu.make_async_copy(far.at[b, pair], ops.at[b, pair], op_sem.at[b, p])

    def for_pairs(b, act):
        number = shape_of(b)[0]
        for p in range(entries // 2):

            @pl.when(number > p)
            def _(p=p):
                act(fetch(b, p))

    def shape_of(b):
        live, top = 0, -1
        for k in range(entries):
            live = live + (cols[b, k] >= 0).astype(jnp.int32)
            top = jnp.maximum(top, cols[b, k])
        return (live + 1) // 2, (top >= owned) if late else (top < owned)

    if begin:

        @pl.loop(0, owned)
        def _(b):
            for_pairs(b, lambda copy: copy.start())

        lay_out_facts(facts, aux, gauges)

    first = gauges[1:2, here]
    active = jnp.where(
        jnp.logical_and(first <= step, step < first + gauges[2:3, here]), gauges[3:4, here], 0.0
    )
    own_cells = lax.broadcasted_iota(jnp.int32, (cells, width), 0)

    def finish(b, total):
        wet = aux[b, :, 0:1]
        where = gauges[0:1, here].astype(jnp.int32) - (position * owned + b) * cells
        source = jnp.where(own_cells == where, active, 0.0)
        gathered = None
        for c in range(3):
            band = pl.ds(c * cells, cells)
            before = lam[b, band, here].astype(jnp.float32)
            updated = wet * (before + total[c * cells : (c + 1) * cells])
            if c == 0:
                updated = updated + source
            updated = updated.astype(jnp.bfloat16)
            new[b, band, here] = updated
            if last:
                term = aux[b, :, 1 + c : 2 + c] * before
                gathered = term if gathered is None else gathered + term
                gathered = gathered + aux[b, :, 4 + c : 5 + c] * updated.astype(jnp.float32)
        if last:
            raw[b, :, here] = gathered
            more = jnp.sum(gathered * gathered, axis=0, keepdims=True)[None]
            squares[:, :, here] += jnp.broadcast_to(more, (squares.shape[0], 1, width))

    def picked(b, k):
        col = cols[b, k]
        block = lam[jnp.clip(col, 0, owned - 1), :, here]
        if late:
            block = jnp.where(col < owned, block, slots[jnp.maximum(col - owned, 0)])
        return jnp.where(col >= 0, block, jnp.zeros_like(block))

    def make_row(b, n):
        state = [lam[b, :, here]] + [picked(b, k) for k in range(1, 2 * n)]
        weights = jnp.concatenate([ops[b, k] for k in range(2 * n)], axis=1)
        total = jnp.dot(
            weights, jnp.concatenate(state, axis=0), preferred_element_type=jnp.float32
        )
        finish(b, total)

    def each_row():
        @pl.loop(0, owned)
        def _(b):
            pairs, mine = shape_of(b)
            if begin:
                for_pairs(b, lambda copy: copy.wait())
            for n in range(1, entries // 2 + 1):

                @pl.when(jnp.logical_and(mine, pairs == n))
                def _(n=n):
                    make_row(b, n)

    if late:
        plain = True
        for b in range(owned):
            pairs, mine = shape_of(b)
            plain = jnp.logical_and(plain, jnp.logical_and(mine, pairs == 1))

        @pl.when(plain)
        def _():
            for b in range(owned):
                make_row(b, 1)

        @pl.when(jnp.logical_not(plain))
        def _():
            each_row()
    else:
        each_row()

    if sends:
        groups = send_groups(position)
        for r in ROUTES:
            for c in range(2):
                sends[r][c] = new[jnp.maximum(halo[0, c, groups[r]], 0), :, here]


def step_rows(late, last, step, part, final, cost, inputs, lam, received=None, before=None):
    cols, halo, ops, facts = inputs
    owned, rows, width = lam.shape
    cells = rows // 3
    devices = lax.axis_size("dom")
    smem, vmem = (pl.BlockSpec(memory_space=m) for m in (pltpu.SMEM, pltpu.VMEM))
    begin = not late and step == 0
    args = [cols, halo, pinned(lam), in_hbm(ops) if begin else pinned(ops), *facts]
    aliases = {}
    if late:
        args += [pinned(received[r]) for r in ROUTES]
        for i in range(1 + last):
            aliases[len(args)] = i
            args.append(pinned(before[i]))
        if last:
            args.append(before[2])
    out_shape = [pltpu.VMEM(lam.shape, lam.dtype)]
    if last:
        out_shape += [
            pltpu.VMEM((owned, cells, width), jnp.float32),
            pltpu.VMEM((devices if final else 1, 1, width), jnp.float32),
        ]
    elif late:
        out_shape += [pltpu.VMEM((2, rows, part[1]), lam.dtype)] * 4
    scratch = [pltpu.VMEM((owned, rows, part[1]), lam.dtype)] if late else []
    if begin:
        scratch = [pltpu.SemaphoreType.DMA((owned, ops.shape[1] // 2))]
        out_shape += [
            pltpu.VMEM((owned, cells, 2 + 3 * 2), jnp.float32),
            pltpu.VMEM((4, width), jnp.float32),
            pltpu.VMEM(ops.shape, ops.dtype),
        ]
    return pl.pallas_call(
        functools.partial(step_kernel, late, last, step, part, final),
        name=("late" if late else "early") + "_rows",
        out_shape=out_shape,
        in_specs=[smem, smem, vmem, pl.BlockSpec(memory_space=pltpu.HBM) if begin else vmem]
        + [vmem] * (len(args) - 4),
        out_specs=[vmem] * len(out_shape),
        input_output_aliases=aliases,
        scratch_shapes=scratch,
        compiler_params=pltpu.CompilerParams(vmem_limit_bytes=16 * 1024 * 1024),
        cost_estimate=pl.CostEstimate(flops=0, bytes_accessed=cost, transcendentals=0),
    )(*args)


def scale_kernel(cells_total, sums, raw, out, scaled_rows, sems):
    factor = lax.rsqrt(jnp.sum(sums[...], axis=0) / cells_total + 1e-06)
    copies = []
    for b in range(raw.shape[0]):
        scaled_rows[b] = raw[b] * factor
        copies.append(pltpu.make_async_copy(scaled_rows.at[b], out.at[b], sems.at[b]))
        copies[b].start()
    for copy in copies:
        copy.wait()


def scaled(sums, raw, cells_total):
    vmem = pl.BlockSpec(memory_space=pltpu.VMEM)
    return pl.pallas_call(
        functools.partial(scale_kernel, cells_total),
        name="scale",
        out_shape=jax.ShapeDtypeStruct(raw.shape, raw.dtype),
        in_specs=[vmem, vmem],
        out_specs=pl.BlockSpec(memory_space=pltpu.HBM),
        scratch_shapes=[
            pltpu.VMEM(raw.shape, raw.dtype),
            pltpu.SemaphoreType.DMA((raw.shape[0],)),
        ],
        compiler_params=pltpu.CompilerParams(vmem_limit_bytes=8 * 1024 * 1024),
    )(sums, pinned(raw))


def per_device(
    adjoint_end,
    operator_blocks,
    block_cols,
    halo_send,
    wet_cells,
    gauge_cells,
    window_first,
    window_len,
    gauge_gain,
    snapshots,
):
    owned, cells = wet_cells.shape
    steps = snapshots.shape[0]
    devices = lax.axis_size("dom")
    halo = jnp.swapaxes(halo_send, 1, 2)
    facts = [wet_cells, snapshots] + [
        v[None] for v in (gauge_cells, window_first, window_len, gauge_gain)
    ]
    width = adjoint_end.shape[2]
    parts = [(at, width // PARTS) for at in range(0, width, width // PARTS)]
    lam = adjoint_end
    received = [
        exchange(pick_sends(part, cost, halo, lam)) for part, cost in zip(parts, PICK_COST)
    ]
    for step in range(steps):
        last = step == steps - 1
        inputs = (block_cols, halo, operator_blocks, facts)
        state = step_rows(False, last, step, (0, width), False, EARLY_COST, inputs, lam)
        if step == 0:
            *state, aux, gauges, operator_blocks = state
            facts = [aux, gauges]
            inputs = (block_cols, halo, operator_blocks, facts)
        arriving, received = received, []
        for i, part in enumerate(parts):
            final = last and i == len(parts) - 1
            state = step_rows(
                True, last, step, part, final, LATE_COST[step][i], inputs, lam, arriving[i], state
            )
            if not last:
                received.append(exchange(dict(zip(ROUTES, state[1:]))))
        lam = state[0]
    raw, squares = state[1:]
    sums = lax.all_to_all(squares, "dom", 0, 0, tiled=True)
    return (lam, scaled(sums, raw, devices * owned * cells))


def solution(mesh):
    return jax.shard_map(
        per_device,
        mesh=mesh,
        in_specs=(
            P("dom", None, None),
            P("dom", None, None, None),
            P("dom", None),
            P("dom", None, None),
            P("dom", None),
            P(),
            P(),
            P(),
            P(),
            P(None, "dom", None),
        ),
        out_specs=(P("dom", None, None), P("dom", None, None)),
        check_vma=False,
    )
```

```python
import functools

import jax
import jax.numpy as jnp
from jax import lax
from jax.experimental import pallas as pl
from jax.experimental.pallas import tpu as pltpu
from jax.sharding import PartitionSpec as P

PARTS = 2
PICK_COST = 4 << 20
EARLY_COST = 4 << 20
LATE_COST = ((4 << 20, 4 << 20), (4 << 20, 4 << 20))
ROUTES = ("inner", "outer", "cross", "swap")


def route_pairs(devices):
    swap = [(i, i ^ 1) for i in range(devices)]
    cross = [(i, i + 1) for i in range(1, devices - 1, 2)]
    inner = [(i, i ^ 2) for i in range(devices)]
    outer = [(i, i + 2) for i in range(devices - 2) if i & 2]
    both = lambda pairs: pairs + [(j, i) for i, j in pairs]
    return dict(swap=swap, cross=both(cross), inner=inner, outer=both(outer))


def send_groups(device):
    core, chip = device % 2, (device // 2) % 2
    return dict(swap=2 - core, cross=1 + core, inner=3 - 3 * chip, outer=3 * chip)


def receive_groups(device):
    core, chip = device % 2, (device // 2) % 2
    return dict(swap=1 + core, cross=2 - core, inner=3 * chip, outer=3 - 3 * chip)


def exchange(sends):
    pairs = route_pairs(lax.axis_size("dom"))
    return {r: lax.ppermute(sends[r], "dom", pairs[r]) for r in ROUTES}


def pinned(value):
    return pltpu.with_memory_space_constraint(value, pltpu.VMEM)


def in_hbm(value):
    return pltpu.with_memory_space_constraint(value, pltpu.HBM)


def pick_kernel(part, halo, lam, *rest):
    outs, sems = dict(zip(ROUTES, rest[:4])), rest[4]
    groups = send_groups(lax.axis_index("dom"))
    copies = []
    for i, r in enumerate(ROUTES):
        for c in range(2):
            row = jnp.maximum(halo[0, c, groups[r]], 0)
            copies.append(
                pltpu.make_async_copy(lam.at[row, :, pl.ds(*part)], outs[r].at[c], sems.at[i, c])
            )
    for copy in copies:
        copy.start()
    for copy in copies:
        copy.wait()


def pick_sends(part, cost, place, halo, lam):
    sent = pltpu.VMEM((2, lam.shape[1], part[1]), lam.dtype)
    outs = pl.pallas_call(
        functools.partial(pick_kernel, part),
        name="pick_sends",
        out_shape=[sent] * 4,
        in_specs=[pl.BlockSpec(memory_space=pltpu.SMEM), pl.BlockSpec(memory_space=place)],
        out_specs=[pl.BlockSpec(memory_space=pltpu.VMEM)] * 4,
        scratch_shapes=[pltpu.SemaphoreType.DMA((4, 2))],
        compiler_params=pltpu.CompilerParams(vmem_limit_bytes=4 * 1024 * 1024),
        cost_estimate=pl.CostEstimate(flops=0, bytes_accessed=cost, transcendentals=0),
    )(in_hbm(halo), pltpu.with_memory_space_constraint(lam, place))
    return dict(zip(ROUTES, outs))


def lay_out_facts(facts, aux, gauges):
    wet, snapshots = facts[:2]
    owned, cells = wet.shape
    for i, fact in enumerate(facts[2:]):
        gauges[i : i + 1, :] = fact[...].astype(jnp.float32)
    for b in range(owned):
        rows = [wet[b : b + 1, :].astype(jnp.float32)]
        for t in range(snapshots.shape[0]):
            for c in range(3):
                rows.append(snapshots[t, b : b + 1, c * cells : (c + 1) * cells])
        rows.append(jnp.zeros((1, cells), jnp.float32))
        aux[b] = jnp.concatenate(rows, axis=0).T


def step_kernel(late, last, step, part, final, *refs):
    refs = list(refs)
    take = lambda n: [refs.pop(0) for _ in range(n)]
    cols, halo, lam, ops = take(4)
    begin = not late and step == 0
    facts = take(6) if begin else None
    aux, gauges = (None, None) if begin else take(2)
    received = take(4) if late else []
    take(1 + last if late else 0)
    done_squares = take(1)[0] if late and last else None
    (new,) = take(1)
    raw, squares = take(2) if last else (None, None)
    sends = dict(zip(ROUTES, take(4))) if late and not last else {}
    if begin:
        aux, gauges, kept, kept_cols, kept_halo = take(5)
        ahead = [dict(zip(ROUTES, take(4))) for _ in range(PARTS - 1)]
        far, ops = ops, kept
    order = refs.pop(0)
    (slots,) = refs if late else (None,)
    (op_sem,) = refs if begin else (None,)

    owned, entries = ops.shape[0], ops.shape[1]
    rows, width = lam.shape[1], part[1]
    cells = rows // 3
    here = pl.ds(*part)
    position = lax.axis_index("dom")

    def sent_rows():
        groups = send_groups(position)
        return [(r, c, jnp.maximum(halo[0, c, groups[r]], 0)) for r in ROUTES for c in range(2)]

    if late:
        groups = receive_groups(position)
        for i, r in enumerate(ROUTES):
            slots[pl.ds(2 * groups[r], 2)] = received[i][...]
    if last:
        if late:
            squares[...] = jnp.broadcast_to(done_squares[...], squares.shape)
        else:
            squares[...] = jnp.zeros(squares.shape, jnp.float32)

    def fetch(b, p):
        pair = pl.ds(2 * p, 2)
        return pltpu.make_async_copy(far.at[b, pair], ops.at[b, pair], op_sem.at[b, p])

    def for_pairs(b, act):
        number = shape_of(b)[0]
        for p in range(entries // 2):

            @pl.when(number > p)
            def _(p=p):
                act(fetch(b, p))

    def shape_of(b):
        live, top = 0, -1
        for k in range(entries):
            live = live + (cols[b, k] >= 0).astype(jnp.int32)
            top = jnp.maximum(top, cols[b, k])
        return (live + 1) // 2, (top >= owned) if late else (top < owned)

    if begin:

        for own in (True, False):

            @pl.loop(0, owned)
            def _(b, own=own):
                @pl.when(shape_of(b)[1] == own)
                def _():
                    for_pairs(b, lambda copy: copy.start())

        lay_out_facts(facts, aux, gauges)
        for b in range(owned):
            for k in range(entries):
                kept_cols[b, k] = cols[b, k]
        for c in range(halo.shape[1]):
            for o in range(halo.shape[2]):
                kept_halo[0, c, o] = halo[0, c, o]
        for i, picks in enumerate(ahead):
            band = pl.ds((i + 1) * (part[1] // PARTS), part[1] // PARTS)
            for r, c, row in sent_rows():
                picks[r][c] = lam[row, :, band]

    first = gauges[1:2, here]
    active = jnp.where(
        jnp.logical_and(first <= step, step < first + gauges[2:3, here]), gauges[3:4, here], 0.0
    )
    own_cells = lax.broadcasted_iota(jnp.int32, (cells, width), 0)

    def finish(b, total, counted=None):
        wet = aux[b, :, 0:1]
        where = gauges[0:1, here].astype(jnp.int32) - (position * owned + b) * cells
        source = jnp.where(own_cells == where, active, 0.0)
        gathered = None
        for c in range(3):
            band = pl.ds(c * cells, cells)
            before = lam[b, band, here].astype(jnp.float32)
            updated = wet * (before + total[c * cells : (c + 1) * cells])
            if c == 0:
                updated = updated + source
            updated = updated.astype(jnp.bfloat16)
            new[b, band, here] = updated
            if last:
                term = aux[b, :, 1 + c : 2 + c] * before
                gathered = term if gathered is None else gathered + term
                gathered = gathered + aux[b, :, 4 + c : 5 + c] * updated.astype(jnp.float32)
        if last:
            raw[b, :, here] = gathered
            more = jnp.sum(gathered * gathered, axis=0, keepdims=True)[None]
            if counted is not None:
                more = more * counted
            squares[:, :, here] += jnp.broadcast_to(more, (squares.shape[0], 1, width))

    def picked(b, k):
        col = cols[b, k]
        block = lam[jnp.clip(col, 0, owned - 1), :, here]
        if late:
            block = jnp.where(col < owned, block, slots[jnp.maximum(col - owned, 0)])
        return jnp.where(col >= 0, block, jnp.zeros_like(block))

    def row_total(b, n):
        state = [lam[b, :, here]] + [picked(b, k) for k in range(1, 2 * n)]
        weights = jnp.concatenate([ops[b, k] for k in range(2 * n)], axis=1)
        return jnp.dot(
            weights, jnp.concatenate(state, axis=0), preferred_element_type=jnp.float32
        )

    def by_twos():
        for n in range(1, entries // 2 + 1):
            count = 0
            for b in range(owned):
                pairs, mine = shape_of(b)
                order[n - 1, count] = b
                count = count + jnp.logical_and(mine, pairs == n).astype(jnp.int32)

            @pl.loop(0, (count + 1) // 2)
            def _(i, n=n, count=count):
                b, other = order[n - 1, 2 * i], order[n - 1, jnp.minimum(2 * i + 1, count - 1)]
                if begin:
                    for p in range(n):
                        fetch(b, p).wait()

                    @pl.when(other != b)
                    def _():
                        for p in range(n):
                            fetch(other, p).wait()

                total, ahead = row_total(b, n), row_total(other, n)
                finish(b, total)
                finish(other, ahead, jnp.where(other != b, 1.0, 0.0))

    if late:
        plain = True
        for b in range(owned):
            pairs, mine = shape_of(b)
            plain = jnp.logical_and(plain, jnp.logical_and(mine, pairs == 1))

        @pl.when(plain)
        def _():
            total = row_total(0, 1)
            for b in range(owned):
                ahead = row_total(b + 1, 1) if b + 1 < owned else None
                finish(b, total)
                total = ahead

        @pl.when(jnp.logical_not(plain))
        def _():
            by_twos()
    else:
        by_twos()

    if begin:

        @pl.loop(0, owned)
        def _(b):
            @pl.when(jnp.logical_not(shape_of(b)[1]))
            def _():
                for_pairs(b, lambda copy: copy.wait())

    if sends:
        for r, c, row in sent_rows():
            sends[r][c] = new[row, :, here]


def step_rows(late, last, step, part, final, cost, inputs, lam, received=None, before=None):
    cols, halo, ops, facts = inputs
    owned, rows, width = lam.shape
    cells = rows // 3
    devices = lax.axis_size("dom")
    smem, vmem = (pl.BlockSpec(memory_space=m) for m in (pltpu.SMEM, pltpu.VMEM))
    begin = not late and step == 0
    args = [in_hbm(cols) if begin else cols, halo, pinned(lam), in_hbm(ops) if begin else pinned(ops), *facts]
    aliases = {}
    if late:
        args += [pinned(received[r]) for r in ROUTES]
        for i in range(1 + last):
            aliases[len(args)] = i
            args.append(pinned(before[i]))
        if last:
            args.append(before[2])
    out_shape = [pltpu.VMEM(lam.shape, lam.dtype)]
    if last:
        out_shape += [
            pltpu.VMEM((owned, cells, width), jnp.float32),
            pltpu.VMEM((devices if final else 1, 1, width), jnp.float32),
        ]
    elif late:
        out_shape += [pltpu.VMEM((2, rows, part[1]), lam.dtype)] * 4
    scratch = [pltpu.SMEM((ops.shape[1] // 2, owned), jnp.int32)]
    if late:
        scratch += [pltpu.VMEM((owned, rows, part[1]), lam.dtype)]
    if begin:
        scratch += [pltpu.SemaphoreType.DMA((owned, ops.shape[1] // 2))]
        out_shape += [
            pltpu.VMEM((owned, cells, 2 + 3 * 2), jnp.float32),
            pltpu.VMEM((4, width), jnp.float32),
            pltpu.VMEM(ops.shape, ops.dtype),
            pltpu.SMEM(cols.shape, cols.dtype),
            pltpu.SMEM(halo.shape, halo.dtype),
        ] + [pltpu.VMEM((2, rows, width // PARTS), lam.dtype)] * (4 * (PARTS - 1))
    return pl.pallas_call(
        functools.partial(step_kernel, late, last, step, part, final),
        name=("late" if late else "early") + "_rows",
        out_shape=out_shape,
        in_specs=[smem, smem, vmem, pl.BlockSpec(memory_space=pltpu.HBM) if begin else vmem]
        + [vmem] * (len(args) - 4),
        out_specs=[smem if o.memory_space == pltpu.SMEM else vmem for o in out_shape],
        input_output_aliases=aliases,
        scratch_shapes=scratch,
        compiler_params=pltpu.CompilerParams(vmem_limit_bytes=16 * 1024 * 1024),
        cost_estimate=pl.CostEstimate(flops=0, bytes_accessed=cost, transcendentals=0),
    )(*args)


def scale_kernel(cells_total, sums, raw, out, scaled_rows, sems):
    factor = lax.rsqrt(jnp.sum(sums[...], axis=0) / cells_total + 1e-06)
    copies = []
    for b in range(raw.shape[0]):
        scaled_rows[b] = raw[b] * factor
        copies.append(pltpu.make_async_copy(scaled_rows.at[b], out.at[b], sems.at[b]))
        copies[b].start()
    for copy in copies:
        copy.wait()


def scaled(sums, raw, cells_total):
    vmem = pl.BlockSpec(memory_space=pltpu.VMEM)
    return pl.pallas_call(
        functools.partial(scale_kernel, cells_total),
        name="scale",
        out_shape=jax.ShapeDtypeStruct(raw.shape, raw.dtype),
        in_specs=[vmem, vmem],
        out_specs=pl.BlockSpec(memory_space=pltpu.HBM),
        scratch_shapes=[
            pltpu.VMEM(raw.shape, raw.dtype),
            pltpu.SemaphoreType.DMA((raw.shape[0],)),
        ],
        compiler_params=pltpu.CompilerParams(vmem_limit_bytes=8 * 1024 * 1024),
    )(sums, pinned(raw))


def per_device(
    adjoint_end,
    operator_blocks,
    block_cols,
    halo_send,
    wet_cells,
    gauge_cells,
    window_first,
    window_len,
    gauge_gain,
    snapshots,
):
    owned, cells = wet_cells.shape
    steps = snapshots.shape[0]
    devices = lax.axis_size("dom")
    halo = jnp.swapaxes(halo_send, 1, 2)
    facts = [wet_cells, snapshots] + [
        v[None] for v in (gauge_cells, window_first, window_len, gauge_gain)
    ]
    width = adjoint_end.shape[2]
    parts = [(at, width // PARTS) for at in range(0, width, width // PARTS)]
    lam = adjoint_end
    received = [exchange(pick_sends(parts[0], PICK_COST, pltpu.HBM, halo, lam))]
    for step in range(steps):
        last = step == steps - 1
        inputs = (block_cols, halo, operator_blocks, facts)
        state = step_rows(False, last, step, (0, width), False, EARLY_COST, inputs, lam)
        if step == 0:
            state, (aux, gauges, *kept), picks = state[:1], state[1:6], state[6:]
            operator_blocks, block_cols, halo = kept
            received += [exchange(dict(zip(ROUTES, picks[i : i + 4]))) for i in range(0, len(picks), 4)]
            facts = [aux, gauges]
            inputs = (block_cols, halo, operator_blocks, facts)
        arriving, received = received, []
        for i, part in enumerate(parts):
            final = last and i == len(parts) - 1
            state = step_rows(
                True, last, step, part, final, LATE_COST[step][i], inputs, lam, arriving[i], state
            )
            if not last:
                received.append(exchange(dict(zip(ROUTES, state[1:]))))
        lam = state[0]
    raw, squares = state[1:]
    sums = lax.all_to_all(squares, "dom", 0, 0, tiled=True)
    return (lam, scaled(sums, raw, devices * owned * cells))


def solution(mesh):
    return jax.shard_map(
        per_device,
        mesh=mesh,
        in_specs=(
            P("dom", None, None),
            P("dom", None, None, None),
            P("dom", None),
            P("dom", None, None),
            P("dom", None),
            P(),
            P(),
            P(),
            P(),
            P(None, "dom", None),
        ),
        out_specs=(P("dom", None, None), P("dom", None, None)),
        check_vma=False,
    )
```

```python
import functools

import jax
import jax.numpy as jnp
from jax import lax
from jax.experimental import pallas as pl
from jax.experimental.pallas import tpu as pltpu
from jax.sharding import PartitionSpec as P

PARTS = 2
PICK_COST = 4 << 20
EARLY_COST = 4 << 20
LATE_COST = ((4 << 20, 4 << 20), (4 << 20, 4 << 20))
SPLIT = ("inner", "outer", "cross")
FIRST = ("swap",) + SPLIT
ROUTES = ("swap",) + SPLIT


def route_pairs(devices):
    swap = [(i, i ^ 1) for i in range(devices)]
    cross = [(i, i + 1) for i in range(1, devices - 1, 2)]
    inner = [(i, i ^ 2) for i in range(devices)]
    outer = [(i, i + 2) for i in range(devices - 2) if i & 2]
    both = lambda pairs: pairs + [(j, i) for i, j in pairs]
    return dict(swap=swap, cross=both(cross), inner=inner, outer=both(outer))


def send_groups(device):
    core, chip = device % 2, (device // 2) % 2
    return dict(swap=2 - core, cross=1 + core, inner=3 - 3 * chip, outer=3 * chip)


def receive_groups(device):
    core, chip = device % 2, (device // 2) % 2
    return dict(swap=1 + core, cross=2 - core, inner=3 * chip, outer=3 - 3 * chip)


def exchange(sends):
    pairs = route_pairs(lax.axis_size("dom"))
    return {r: lax.ppermute(sent, "dom", pairs[r]) for r, sent in sends.items()}


def pinned(value):
    return pltpu.with_memory_space_constraint(value, pltpu.VMEM)


def in_hbm(value):
    return pltpu.with_memory_space_constraint(value, pltpu.HBM)


def pick_kernel(part, halo, lam, *rest):
    outs, sems = dict(zip(FIRST, rest[:4])), rest[4]
    groups = send_groups(lax.axis_index("dom"))
    copies = []
    for i, r in enumerate(FIRST):
        band = pl.ds(*(part if r in SPLIT else (0, lam.shape[2])))
        for c in range(2):
            row = jnp.maximum(halo[0, c, groups[r]], 0)
            copies.append(
                pltpu.make_async_copy(lam.at[row, :, band], outs[r].at[c], sems.at[i, c])
            )
    for copy in copies:
        copy.start()
    for copy in copies:
        copy.wait()


def pick_sends(part, cost, place, halo, lam):
    outs = pl.pallas_call(
        functools.partial(pick_kernel, part),
        name="pick_sends",
        out_shape=[
            pltpu.VMEM((2, lam.shape[1], part[1] if r in SPLIT else lam.shape[2]), lam.dtype)
            for r in FIRST
        ],
        in_specs=[pl.BlockSpec(memory_space=pltpu.SMEM), pl.BlockSpec(memory_space=place)],
        out_specs=[pl.BlockSpec(memory_space=pltpu.VMEM)] * 4,
        scratch_shapes=[pltpu.SemaphoreType.DMA((4, 2))],
        compiler_params=pltpu.CompilerParams(vmem_limit_bytes=4 * 1024 * 1024),
        cost_estimate=pl.CostEstimate(flops=0, bytes_accessed=cost, transcendentals=0),
    )(in_hbm(halo), pltpu.with_memory_space_constraint(lam, place))
    return dict(zip(FIRST, outs))


def lay_out_facts(facts, aux, gauges):
    wet, snapshots = facts[:2]
    owned, cells = wet.shape
    for i, fact in enumerate(facts[2:]):
        gauges[i : i + 1, :] = fact[...].astype(jnp.float32)
    for b in range(owned):
        rows = [wet[b : b + 1, :].astype(jnp.float32)]
        for t in range(snapshots.shape[0]):
            for c in range(3):
                rows.append(snapshots[t, b : b + 1, c * cells : (c + 1) * cells])
        rows.append(jnp.zeros((1, cells), jnp.float32))
        aux[b] = jnp.concatenate(rows, axis=0).T


def step_kernel(late, last, step, part, final, *refs):
    refs = list(refs)
    take = lambda n: [refs.pop(0) for _ in range(n)]
    cols, halo, lam, ops = take(4)
    begin = not late and step == 0
    facts = take(6) if begin else None
    aux, gauges = (None, None) if begin else take(2)
    received = dict(zip(ROUTES, take(4))) if late else {}
    take(1 + last if late else 0)
    done_squares = take(1)[0] if late and last else None
    base = take(1)[0] if late and last else None
    (new,) = take(1)
    raw, squares = take(2) if last else (None, None)
    base = take(1)[0] if last and not late else base
    sends = dict(zip(ROUTES, take(4))) if late and not last else {}
    if begin:
        aux, gauges, kept, kept_cols, kept_halo = take(5)
        ahead = [dict(zip(SPLIT, take(3))) for _ in range(PARTS - 1)]
        far, ops = ops, kept
    order = refs.pop(0)
    summed = refs.pop(0) if last else None
    (slots,) = refs if late else (None,)
    (op_sem,) = refs if begin else (None,)

    owned, entries = ops.shape[0], ops.shape[1]
    rows, width = lam.shape[1], part[1]
    cells = rows // 3
    here = pl.ds(*part)
    position = lax.axis_index("dom")

    def sent_rows(routes):
        groups = send_groups(position)
        return [(r, c, jnp.maximum(halo[0, c, groups[r]], 0)) for r in routes for c in range(2)]

    if late:
        groups = receive_groups(position)
        for r in ROUTES:
            slots[pl.ds(2 * groups[r], 2)] = (
                received[r][:, :, here] if r == "swap" and step == 0 else received[r][...]
            )
    if last:
        summed[...] = jnp.zeros(summed.shape, jnp.float32)

    def fetch(b, p):
        pair = pl.ds(2 * p, 2)
        return pltpu.make_async_copy(far.at[b, pair], ops.at[b, pair], op_sem.at[b, p])

    def for_pairs(b, act):
        number = shape_of(b)[0]
        for p in range(entries // 2):

            @pl.when(number > p)
            def _(p=p):
                act(fetch(b, p))

    def shape_of(b):
        live, top = 0, -1
        for k in range(entries):
            live = live + (cols[b, k] >= 0).astype(jnp.int32)
            top = jnp.maximum(top, cols[b, k])
        return (live + 1) // 2, (top >= owned) if late else (top < owned)

    if begin:

        for own in (True, False):

            @pl.loop(0, owned)
            def _(b, own=own):
                @pl.when(shape_of(b)[1] == own)
                def _():
                    for_pairs(b, lambda copy: copy.start())

        lay_out_facts(facts, aux, gauges)
        for b in range(owned):
            for k in range(entries):
                kept_cols[b, k] = cols[b, k]
        for c in range(halo.shape[1]):
            for o in range(halo.shape[2]):
                kept_halo[0, c, o] = halo[0, c, o]
        for i, picks in enumerate(ahead):
            band = pl.ds((i + 1) * (part[1] // PARTS), part[1] // PARTS)
            for r, c, row in sent_rows(SPLIT):
                picks[r][c] = lam[row, :, band]

    first = gauges[1:2, here]
    active = jnp.where(
        jnp.logical_and(first <= step, step < first + gauges[2:3, here]), gauges[3:4, here], 0.0
    )
    own_cells = lax.broadcasted_iota(jnp.int32, (cells, width), 0)

    def prepare(b, total):
        base[b] = lam[b, :, here].astype(jnp.float32) + total
        raw[b, :, here] = from_snapshot(0, b, lambda c: lam[b, pl.ds(c * cells, cells), here])

    def from_snapshot(t, b, state, gathered=None):
        for c in range(3):
            column = 1 + 3 * t + c
            term = aux[b, :, column : column + 1] * state(c).astype(jnp.float32)
            gathered = term if gathered is None else gathered + term
        return gathered

    def finish(b, total, counted=None):
        wet = aux[b, :, 0:1]
        where = gauges[0:1, here].astype(jnp.int32) - (position * owned + b) * cells
        source = jnp.where(own_cells == where, active, 0.0)
        made = []
        for c in range(3):
            band = pl.ds(c * cells, cells)
            if base is not None and late:
                before = base[b, band, here]
            else:
                before = lam[b, band, here].astype(jnp.float32)
            updated = wet * (before + total[c * cells : (c + 1) * cells])
            if c == 0:
                updated = updated + source
            made.append(updated.astype(jnp.bfloat16))
            new[b, band, here] = made[c]
        if last:
            if late:
                gathered = raw[b, :, here]
            else:
                gathered = from_snapshot(0, b, lambda c: lam[b, pl.ds(c * cells, cells), here])
            gathered = from_snapshot(1, b, lambda c: made[c], gathered)
            raw[b, :, here] = gathered
            square = gathered * gathered
            if counted is not None:
                square = square * counted
            summed[...] += sum(square[i : i + 8] for i in range(0, cells, 8))

    def picked(b, k, local=True, received=late):
        col = cols[b, k]
        nothing = jnp.zeros((rows, width), lam.dtype)
        block = nothing
        if received:
            block = jnp.where(col >= owned, slots[jnp.maximum(col - owned, 0)], nothing)
        if local:
            own = lam[jnp.clip(col, 0, owned - 1), :, here]
            block = jnp.where(jnp.logical_and(col >= 0, col < owned), own, block)
        return block

    def row_total(b, entries_of, **kinds):
        state = [
            lam[b, :, here] if k == 0 and kinds.get("local", True) else picked(b, k, **kinds)
            for k in entries_of
        ]
        weights = jnp.concatenate([ops[b, k] for k in entries_of], axis=1)
        return jnp.dot(
            weights, jnp.concatenate(state, axis=0), preferred_element_type=jnp.float32
        )

    def by_twos():
        for n in range(1, entries // 2 + 1):
            count = 0
            for b in range(owned):
                pairs, mine = shape_of(b)
                order[n - 1, count] = b
                count = count + jnp.logical_and(mine, pairs == n).astype(jnp.int32)

            @pl.loop(0, (count + 1) // 2)
            def _(i, n=n, count=count):
                b, other = order[n - 1, 2 * i], order[n - 1, jnp.minimum(2 * i + 1, count - 1)]
                if begin:
                    for p in range(n):
                        fetch(b, p).wait()

                    @pl.when(other != b)
                    def _():
                        for p in range(n):
                            fetch(other, p).wait()

                total, ahead = (row_total(i, range(2 * n)) for i in (b, other))
                finish(b, total)
                finish(other, ahead, jnp.where(other != b, 1.0, 0.0))

    plain = True
    for b in range(owned):
        pairs, mine = shape_of(b)
        plain = jnp.logical_and(plain, jnp.logical_and(mine == late, pairs == 1))

    if late:
        @pl.when(plain)
        def _():
            taken = (1,) if last else (0, 1)
            split = dict(local=not last)
            total = row_total(0, taken, **split)
            for b in range(owned):
                ahead = row_total(b + 1, taken, **split) if b + 1 < owned else None
                finish(b, total)
                total = ahead

        @pl.when(jnp.logical_not(plain))
        def _():
            by_twos()
    else:
        by_twos()

    if last and not late:

        @pl.when(plain)
        def _():
            for b in range(owned):
                prepare(b, row_total(b, (0,)))

        @pl.when(jnp.logical_not(plain))
        def _():
            @pl.loop(0, owned)
            def _(b):
                @pl.when(jnp.logical_not(shape_of(b)[1]))
                def _():
                    prepare(b, 0.0)

    if last:
        sums = jnp.sum(summed[...], axis=0, keepdims=True)[None]
        if late:
            squares[...] = jnp.broadcast_to(done_squares[...], squares.shape)
            sums = sums + done_squares[:, :, here]
        squares[:, :, here] = jnp.broadcast_to(sums, (squares.shape[0], 1, width))

    if begin:

        @pl.loop(0, owned)
        def _(b):
            @pl.when(jnp.logical_not(shape_of(b)[1]))
            def _():
                for_pairs(b, lambda copy: copy.wait())

    if sends:
        for r, c, row in sent_rows(ROUTES):
            sends[r][c] = new[row, :, here]


def step_rows(
    late, last, step, part, final, cost, inputs, lam, received=None, before=None, base=None
):
    cols, halo, ops, facts = inputs
    owned, rows, width = lam.shape
    cells = rows // 3
    devices = lax.axis_size("dom")
    smem, vmem = (pl.BlockSpec(memory_space=m) for m in (pltpu.SMEM, pltpu.VMEM))
    begin = not late and step == 0
    args = [in_hbm(cols) if begin else cols, halo, pinned(lam), in_hbm(ops) if begin else pinned(ops), *facts]
    aliases = {}
    if late:
        args += [pinned(received[r]) for r in ROUTES]
        for i in range(1 + last):
            aliases[len(args)] = i
            args.append(pinned(before[i]))
        if last:
            args += [before[2], pinned(base)]
    out_shape = [pltpu.VMEM(lam.shape, lam.dtype)]
    if last:
        out_shape += [
            pltpu.VMEM((owned, cells, width), jnp.float32),
            pltpu.VMEM((devices if final else 1, 1, width), jnp.float32),
        ]
        if not late:
            out_shape.append(pltpu.VMEM(lam.shape, jnp.float32))
    elif late:
        out_shape += [pltpu.VMEM((2, rows, part[1]), lam.dtype)] * 4
    scratch = [pltpu.SMEM((ops.shape[1] // 2, owned), jnp.int32)]
    if last:
        scratch += [pltpu.VMEM((8, part[1]), jnp.float32)]
    if late:
        scratch += [pltpu.VMEM((owned, rows, part[1]), lam.dtype)]
    if begin:
        scratch += [pltpu.SemaphoreType.DMA((owned, ops.shape[1] // 2))]
        out_shape += [
            pltpu.VMEM((owned, cells, 2 + 3 * 2), jnp.float32),
            pltpu.VMEM((4, width), jnp.float32),
            pltpu.VMEM(ops.shape, ops.dtype),
            pltpu.SMEM(cols.shape, cols.dtype),
            pltpu.SMEM(halo.shape, halo.dtype),
        ] + [pltpu.VMEM((2, rows, width // PARTS), lam.dtype)] * (3 * (PARTS - 1))
    return pl.pallas_call(
        functools.partial(step_kernel, late, last, step, part, final),
        name=("late" if late else "early") + "_rows",
        out_shape=out_shape,
        in_specs=[smem, smem, vmem, pl.BlockSpec(memory_space=pltpu.HBM) if begin else vmem]
        + [vmem] * (len(args) - 4),
        out_specs=[smem if o.memory_space == pltpu.SMEM else vmem for o in out_shape],
        input_output_aliases=aliases,
        scratch_shapes=scratch,
        compiler_params=pltpu.CompilerParams(vmem_limit_bytes=16 * 1024 * 1024),
        cost_estimate=pl.CostEstimate(flops=0, bytes_accessed=cost, transcendentals=0),
    )(*args)


def scale_kernel(cells_total, sums, raw, out, scaled_rows, sems):
    factor = lax.rsqrt(jnp.sum(sums[...], axis=0) / cells_total + 1e-06)
    copies = []
    for b in range(raw.shape[0]):
        scaled_rows[b] = raw[b] * factor
        copies.append(pltpu.make_async_copy(scaled_rows.at[b], out.at[b], sems.at[b]))
        copies[b].start()
    for copy in copies:
        copy.wait()


def scaled(sums, raw, cells_total):
    vmem = pl.BlockSpec(memory_space=pltpu.VMEM)
    return pl.pallas_call(
        functools.partial(scale_kernel, cells_total),
        name="scale",
        out_shape=jax.ShapeDtypeStruct(raw.shape, raw.dtype),
        in_specs=[vmem, vmem],
        out_specs=pl.BlockSpec(memory_space=pltpu.HBM),
        scratch_shapes=[
            pltpu.VMEM(raw.shape, raw.dtype),
            pltpu.SemaphoreType.DMA((raw.shape[0],)),
        ],
        compiler_params=pltpu.CompilerParams(vmem_limit_bytes=8 * 1024 * 1024),
    )(sums, pinned(raw))


def per_device(
    adjoint_end,
    operator_blocks,
    block_cols,
    halo_send,
    wet_cells,
    gauge_cells,
    window_first,
    window_len,
    gauge_gain,
    snapshots,
):
    owned, cells = wet_cells.shape
    steps = snapshots.shape[0]
    devices = lax.axis_size("dom")
    halo = jnp.swapaxes(halo_send, 1, 2)
    facts = [wet_cells, snapshots] + [
        v[None] for v in (gauge_cells, window_first, window_len, gauge_gain)
    ]
    width = adjoint_end.shape[2]
    parts = [(at, width // PARTS) for at in range(0, width, width // PARTS)]
    lam = adjoint_end
    received = [exchange(pick_sends(parts[0], PICK_COST, pltpu.HBM, halo, lam))]
    for step in range(steps):
        last = step == steps - 1
        inputs = (block_cols, halo, operator_blocks, facts)
        state = step_rows(False, last, step, (0, width), False, EARLY_COST, inputs, lam)
        base = None
        if last:
            *state, base = state
        if step == 0:
            state, (aux, gauges, *kept), picks = state[:1], state[1:6], state[6:]
            operator_blocks, block_cols, halo = kept
            received += [exchange(dict(zip(SPLIT, picks[i : i + 3]))) for i in range(0, len(picks), 3)]
            facts = [aux, gauges]
            inputs = (block_cols, halo, operator_blocks, facts)
        if step == 0:
            received[1:] = [some | {"swap": received[0]["swap"]} for some in received[1:]]
        arriving, received = received, []
        for i, part in enumerate(parts):
            final = last and i == len(parts) - 1
            state = step_rows(
                True, last, step, part, final, LATE_COST[step][i], inputs, lam, arriving[i], state, base
            )
            if not last:
                received.append(exchange(dict(zip(ROUTES, state[1:]))))
        lam = state[0]
    raw, squares = state[1:]
    sums = lax.all_to_all(squares, "dom", 0, 0, tiled=True)
    return (lam, scaled(sums, raw, devices * owned * cells))


def solution(mesh):
    return jax.shard_map(
        per_device,
        mesh=mesh,
        in_specs=(
            P("dom", None, None),
            P("dom", None, None, None),
            P("dom", None),
            P("dom", None, None),
            P("dom", None),
            P(),
            P(),
            P(),
            P(),
            P(None, "dom", None),
        ),
        out_specs=(P("dom", None, None), P("dom", None, None)),
        check_vma=False,
    )
```

```python
import functools

import jax
import jax.numpy as jnp
from jax import lax
from jax.experimental import pallas as pl
from jax.experimental.pallas import tpu as pltpu
from jax.sharding import PartitionSpec as P

PARTS = 2
PICK_COST = 4 << 20
EARLY_COST = 4 << 20
LATE_COST = ((4 << 20, 4 << 20), (4 << 20, 4 << 20))
ROUTES = ("inner", "outer", "cross", "swap")


def route_pairs(devices):
    swap = [(i, i ^ 1) for i in range(devices)]
    cross = [(i, i + 1) for i in range(1, devices - 1, 2)]
    inner = [(i, i ^ 2) for i in range(devices)]
    outer = [(i, i + 2) for i in range(devices - 2) if i & 2]
    both = lambda pairs: pairs + [(j, i) for i, j in pairs]
    return dict(swap=swap, cross=both(cross), inner=inner, outer=both(outer))


def send_groups(device):
    core, chip = device % 2, (device // 2) % 2
    return dict(swap=2 - core, cross=1 + core, inner=3 - 3 * chip, outer=3 * chip)


def receive_groups(device):
    core, chip = device % 2, (device // 2) % 2
    return dict(swap=1 + core, cross=2 - core, inner=3 * chip, outer=3 - 3 * chip)


def exchange(sends):
    pairs = route_pairs(lax.axis_size("dom"))
    return {r: lax.ppermute(sends[r], "dom", pairs[r]) for r in ROUTES}


def pinned(value):
    return pltpu.with_memory_space_constraint(value, pltpu.VMEM)


def in_hbm(value):
    return pltpu.with_memory_space_constraint(value, pltpu.HBM)


def pick_kernel(part, halo, lam, *rest):
    outs, sems = dict(zip(ROUTES, rest[:4])), rest[4]
    groups = send_groups(lax.axis_index("dom"))
    copies = []
    for i, r in enumerate(ROUTES):
        for c in range(2):
            row = jnp.maximum(halo[0, c, groups[r]], 0)
            copies.append(
                pltpu.make_async_copy(lam.at[row, :, pl.ds(*part)], outs[r].at[c], sems.at[i, c])
            )
    for copy in copies:
        copy.start()
    for copy in copies:
        copy.wait()


def pick_sends(part, cost, place, halo, lam):
    sent = pltpu.VMEM((2, lam.shape[1], part[1]), lam.dtype)
    outs = pl.pallas_call(
        functools.partial(pick_kernel, part),
        name="pick_sends",
        out_shape=[sent] * 4,
        in_specs=[pl.BlockSpec(memory_space=pltpu.SMEM), pl.BlockSpec(memory_space=place)],
        out_specs=[pl.BlockSpec(memory_space=pltpu.VMEM)] * 4,
        scratch_shapes=[pltpu.SemaphoreType.DMA((4, 2))],
        compiler_params=pltpu.CompilerParams(vmem_limit_bytes=4 * 1024 * 1024),
        cost_estimate=pl.CostEstimate(flops=0, bytes_accessed=cost, transcendentals=0),
    )(in_hbm(halo), pltpu.with_memory_space_constraint(lam, place))
    return dict(zip(ROUTES, outs))


def lay_out_facts(facts, aux, gauges):
    wet, snapshots = facts[:2]
    owned, cells = wet.shape
    for i, fact in enumerate(facts[2:]):
        gauges[i : i + 1, :] = fact[...].astype(jnp.float32)
    for b in range(owned):
        rows = [wet[b : b + 1, :].astype(jnp.float32)]
        for t in range(snapshots.shape[0]):
            for c in range(3):
                rows.append(snapshots[t, b : b + 1, c * cells : (c + 1) * cells])
        rows.append(jnp.zeros((1, cells), jnp.float32))
        aux[b] = jnp.concatenate(rows, axis=0).T


def step_kernel(late, last, step, part, final, *refs):
    refs = list(refs)
    take = lambda n: [refs.pop(0) for _ in range(n)]
    cols, halo, lam, ops = take(4)
    begin = not late and step == 0
    facts = take(6) if begin else None
    aux, gauges = (None, None) if begin else take(2)
    received = take(4) if late else []
    take(1 + last if late else 0)
    done_squares = take(1)[0] if late and last else None
    base = take(1)[0] if late and last else None
    (new,) = take(1)
    raw, squares = take(2) if last else (None, None)
    base = take(1)[0] if last and not late else base
    sends = dict(zip(ROUTES, take(4))) if late and not last else {}
    if begin:
        aux, gauges, kept, kept_cols, kept_halo = take(5)
        ahead = [dict(zip(ROUTES, take(4))) for _ in range(PARTS - 1)]
        far, ops = ops, kept
    order = refs.pop(0)
    summed = refs.pop(0) if last else None
    (slots,) = refs if late else (None,)
    (op_sem,) = refs if begin else (None,)

    owned, entries = ops.shape[0], ops.shape[1]
    rows, width = lam.shape[1], part[1]
    cells = rows // 3
    here = pl.ds(*part)
    position = lax.axis_index("dom")

    def sent_rows():
        groups = send_groups(position)
        return [(r, c, jnp.maximum(halo[0, c, groups[r]], 0)) for r in ROUTES for c in range(2)]

    if late:
        groups = receive_groups(position)
        for i, r in enumerate(ROUTES):
            slots[pl.ds(2 * groups[r], 2)] = received[i][...]
    if last:
        summed[...] = jnp.zeros(summed.shape, jnp.float32)

    def fetch(b, p):
        pair = pl.ds(2 * p, 2)
        return pltpu.make_async_copy(far.at[b, pair], ops.at[b, pair], op_sem.at[b, p])

    def for_pairs(b, act):
        number = shape_of(b)[0]
        for p in range(entries // 2):

            @pl.when(number > p)
            def _(p=p):
                act(fetch(b, p))

    def shape_of(b):
        live, top = 0, -1
        for k in range(entries):
            live = live + (cols[b, k] >= 0).astype(jnp.int32)
            top = jnp.maximum(top, cols[b, k])
        return (live + 1) // 2, (top >= owned) if late else (top < owned)

    if begin:

        for own in (True, False):

            @pl.loop(0, owned)
            def _(b, own=own):
                @pl.when(shape_of(b)[1] == own)
                def _():
                    for_pairs(b, lambda copy: copy.start())

        lay_out_facts(facts, aux, gauges)
        for b in range(owned):
            for k in range(entries):
                kept_cols[b, k] = cols[b, k]
        for c in range(halo.shape[1]):
            for o in range(halo.shape[2]):
                kept_halo[0, c, o] = halo[0, c, o]
        for i, picks in enumerate(ahead):
            band = pl.ds((i + 1) * (part[1] // PARTS), part[1] // PARTS)
            for r, c, row in sent_rows():
                picks[r][c] = lam[row, :, band]

    first = gauges[1:2, here]
    active = jnp.where(
        jnp.logical_and(first <= step, step < first + gauges[2:3, here]), gauges[3:4, here], 0.0
    )
    own_cells = lax.broadcasted_iota(jnp.int32, (cells, width), 0)

    def prepare(b, total):
        base[b] = lam[b, :, here].astype(jnp.float32) + total
        raw[b, :, here] = from_snapshot(0, b, lambda c: lam[b, pl.ds(c * cells, cells), here])

    def from_snapshot(t, b, state, gathered=None):
        for c in range(3):
            column = 1 + 3 * t + c
            term = aux[b, :, column : column + 1] * state(c).astype(jnp.float32)
            gathered = term if gathered is None else gathered + term
        return gathered

    def finish(b, total, counted=None):
        wet = aux[b, :, 0:1]
        where = gauges[0:1, here].astype(jnp.int32) - (position * owned + b) * cells
        source = jnp.where(own_cells == where, active, 0.0)
        made = []
        for c in range(3):
            band = pl.ds(c * cells, cells)
            if base is not None and late:
                before = base[b, band, here]
            else:
                before = lam[b, band, here].astype(jnp.float32)
            updated = wet * (before + total[c * cells : (c + 1) * cells])
            if c == 0:
                updated = updated + source
            made.append(updated.astype(jnp.bfloat16))
            new[b, band, here] = made[c]
        if last:
            if late:
                gathered = raw[b, :, here]
            else:
                gathered = from_snapshot(0, b, lambda c: lam[b, pl.ds(c * cells, cells), here])
            gathered = from_snapshot(1, b, lambda c: made[c], gathered)
            raw[b, :, here] = gathered
            square = gathered * gathered
            if counted is not None:
                square = square * counted
            summed[...] += sum(square[i : i + 8] for i in range(0, cells, 8))

    def picked(b, k, local=True, received=late):
        col = cols[b, k]
        nothing = jnp.zeros((rows, width), lam.dtype)
        block = nothing
        if received:
            block = jnp.where(col >= owned, slots[jnp.maximum(col - owned, 0)], nothing)
        if local:
            own = lam[jnp.clip(col, 0, owned - 1), :, here]
            block = jnp.where(jnp.logical_and(col >= 0, col < owned), own, block)
        return block

    def row_total(b, entries_of, **kinds):
        state = [
            lam[b, :, here] if k == 0 and kinds.get("local", True) else picked(b, k, **kinds)
            for k in entries_of
        ]
        weights = jnp.concatenate([ops[b, k] for k in entries_of], axis=1)
        return jnp.dot(
            weights, jnp.concatenate(state, axis=0), preferred_element_type=jnp.float32
        )

    def by_twos():
        for n in range(1, entries // 2 + 1):
            count = 0
            for b in range(owned):
                pairs, mine = shape_of(b)
                order[n - 1, count] = b
                count = count + jnp.logical_and(mine, pairs == n).astype(jnp.int32)

            @pl.loop(0, (count + 1) // 2)
            def _(i, n=n, count=count):
                b, other = order[n - 1, 2 * i], order[n - 1, jnp.minimum(2 * i + 1, count - 1)]
                if begin:
                    for p in range(n):
                        fetch(b, p).wait()

                    @pl.when(other != b)
                    def _():
                        for p in range(n):
                            fetch(other, p).wait()

                total, ahead = (row_total(i, range(2 * n)) for i in (b, other))
                finish(b, total)
                finish(other, ahead, jnp.where(other != b, 1.0, 0.0))

    plain = True
    for b in range(owned):
        pairs, mine = shape_of(b)
        plain = jnp.logical_and(plain, jnp.logical_and(mine == late, pairs == 1))

    if late:
        @pl.when(plain)
        def _():
            taken = (1,) if last else (0, 1)
            split = dict(local=not last)
            total = row_total(0, taken, **split)
            for b in range(owned):
                ahead = row_total(b + 1, taken, **split) if b + 1 < owned else None
                finish(b, total)
                total = ahead

        @pl.when(jnp.logical_not(plain))
        def _():
            by_twos()
    else:
        by_twos()

    if last and not late:

        @pl.when(plain)
        def _():
            for b in range(owned):
                prepare(b, row_total(b, (0,)))

        @pl.when(jnp.logical_not(plain))
        def _():
            @pl.loop(0, owned)
            def _(b):
                @pl.when(jnp.logical_not(shape_of(b)[1]))
                def _():
                    prepare(b, 0.0)

    if last:
        sums = jnp.sum(summed[...], axis=0, keepdims=True)[None]
        if late:
            squares[...] = jnp.broadcast_to(done_squares[...], squares.shape)
            sums = sums + done_squares[:, :, here]
        squares[:, :, here] = jnp.broadcast_to(sums, (squares.shape[0], 1, width))

    if begin:

        @pl.loop(0, owned)
        def _(b):
            @pl.when(jnp.logical_not(shape_of(b)[1]))
            def _():
                for_pairs(b, lambda copy: copy.wait())

    if sends:
        for r, c, row in sent_rows():
            sends[r][c] = new[row, :, here]


def step_rows(
    late, last, step, part, final, cost, inputs, lam, received=None, before=None, base=None
):
    cols, halo, ops, facts = inputs
    owned, rows, width = lam.shape
    cells = rows // 3
    devices = lax.axis_size("dom")
    smem, vmem = (pl.BlockSpec(memory_space=m) for m in (pltpu.SMEM, pltpu.VMEM))
    begin = not late and step == 0
    args = [in_hbm(cols) if begin else cols, halo, pinned(lam), in_hbm(ops) if begin else pinned(ops), *facts]
    aliases = {}
    if late:
        args += [pinned(received[r]) for r in ROUTES]
        for i in range(1 + last):
            aliases[len(args)] = i
            args.append(pinned(before[i]))
        if last:
            args += [before[2], pinned(base)]
    out_shape = [pltpu.VMEM(lam.shape, lam.dtype)]
    if last:
        out_shape += [
            pltpu.VMEM((owned, cells, width), jnp.float32),
            pltpu.VMEM((devices if final else 1, 1, width), jnp.float32),
        ]
        if not late:
            out_shape.append(pltpu.VMEM(lam.shape, jnp.float32))
    elif late:
        out_shape += [pltpu.VMEM((2, rows, part[1]), lam.dtype)] * 4
    scratch = [pltpu.SMEM((ops.shape[1] // 2, owned), jnp.int32)]
    if last:
        scratch += [pltpu.VMEM((8, part[1]), jnp.float32)]
    if late:
        scratch += [pltpu.VMEM((owned, rows, part[1]), lam.dtype)]
    if begin:
        scratch += [pltpu.SemaphoreType.DMA((owned, ops.shape[1] // 2))]
        out_shape += [
            pltpu.VMEM((owned, cells, 2 + 3 * 2), jnp.float32),
            pltpu.VMEM((4, width), jnp.float32),
            pltpu.VMEM(ops.shape, ops.dtype),
            pltpu.SMEM(cols.shape, cols.dtype),
            pltpu.SMEM(halo.shape, halo.dtype),
        ] + [pltpu.VMEM((2, rows, width // PARTS), lam.dtype)] * (4 * (PARTS - 1))
    return pl.pallas_call(
        functools.partial(step_kernel, late, last, step, part, final),
        name=("late" if late else "early") + "_rows",
        out_shape=out_shape,
        in_specs=[smem, smem, vmem, pl.BlockSpec(memory_space=pltpu.HBM) if begin else vmem]
        + [vmem] * (len(args) - 4),
        out_specs=[smem if o.memory_space == pltpu.SMEM else vmem for o in out_shape],
        input_output_aliases=aliases,
        scratch_shapes=scratch,
        compiler_params=pltpu.CompilerParams(vmem_limit_bytes=16 * 1024 * 1024),
        cost_estimate=pl.CostEstimate(flops=0, bytes_accessed=cost, transcendentals=0),
    )(*args)


def scale_kernel(cells_total, sums, raw, out, scaled_rows, sems):
    factor = lax.rsqrt(jnp.sum(sums[...], axis=0) / cells_total + 1e-06)
    copies = []
    for b in range(raw.shape[0]):
        scaled_rows[b] = raw[b] * factor
        copies.append(pltpu.make_async_copy(scaled_rows.at[b], out.at[b], sems.at[b]))
        copies[b].start()
    for copy in copies:
        copy.wait()


def scaled(sums, raw, cells_total):
    vmem = pl.BlockSpec(memory_space=pltpu.VMEM)
    return pl.pallas_call(
        functools.partial(scale_kernel, cells_total),
        name="scale",
        out_shape=jax.ShapeDtypeStruct(raw.shape, raw.dtype),
        in_specs=[vmem, vmem],
        out_specs=pl.BlockSpec(memory_space=pltpu.HBM),
        scratch_shapes=[
            pltpu.VMEM(raw.shape, raw.dtype),
            pltpu.SemaphoreType.DMA((raw.shape[0],)),
        ],
        compiler_params=pltpu.CompilerParams(vmem_limit_bytes=8 * 1024 * 1024),
    )(sums, pinned(raw))


def per_device(
    adjoint_end,
    operator_blocks,
    block_cols,
    halo_send,
    wet_cells,
    gauge_cells,
    window_first,
    window_len,
    gauge_gain,
    snapshots,
):
    owned, cells = wet_cells.shape
    steps = snapshots.shape[0]
    devices = lax.axis_size("dom")
    halo = jnp.swapaxes(halo_send, 1, 2)
    facts = [wet_cells, snapshots] + [
        v[None] for v in (gauge_cells, window_first, window_len, gauge_gain)
    ]
    width = adjoint_end.shape[2]
    parts = [(at, width // PARTS) for at in range(0, width, width // PARTS)]
    lam = adjoint_end
    received = [exchange(pick_sends(parts[0], PICK_COST, pltpu.HBM, halo, lam))]
    for step in range(steps):
        last = step == steps - 1
        inputs = (block_cols, halo, operator_blocks, facts)
        state = step_rows(False, last, step, (0, width), False, EARLY_COST, inputs, lam)
        base = None
        if last:
            *state, base = state
        if step == 0:
            state, (aux, gauges, *kept), picks = state[:1], state[1:6], state[6:]
            operator_blocks, block_cols, halo = kept
            received += [exchange(dict(zip(ROUTES, picks[i : i + 4]))) for i in range(0, len(picks), 4)]
            facts = [aux, gauges]
            inputs = (block_cols, halo, operator_blocks, facts)
        arriving, received = received, []
        for i, part in enumerate(parts):
            final = last and i == len(parts) - 1
            state = step_rows(
                True, last, step, part, final, LATE_COST[step][i], inputs, lam, arriving[i], state, base
            )
            if not last:
                received.append(exchange(dict(zip(ROUTES, state[1:]))))
        lam = state[0]
    raw, squares = state[1:]
    sums = lax.all_to_all(squares, "dom", 0, 0, tiled=True)
    return (lam, scaled(sums, raw, devices * owned * cells))


def solution(mesh):
    return jax.shard_map(
        per_device,
        mesh=mesh,
        in_specs=(
            P("dom", None, None),
            P("dom", None, None, None),
            P("dom", None),
            P("dom", None, None),
            P("dom", None),
            P(),
            P(),
            P(),
            P(),
            P(None, "dom", None),
        ),
        out_specs=(P("dom", None, None), P("dom", None, None)),
        check_vma=False,
    )
```

```python
import functools

import jax
import jax.numpy as jnp
from jax import lax
from jax.experimental import pallas as pl
from jax.experimental.pallas import tpu as pltpu
from jax.sharding import PartitionSpec as P

PARTS = 2
PICK_COST = 4 << 20
EARLY_COST = 4 << 20
LATE_COST = ((4 << 20, 4 << 20), (4 << 20, 4 << 20))
ROUTES = ("inner", "outer", "cross", "swap")


def route_pairs(devices):
    swap = [(i, i ^ 1) for i in range(devices)]
    cross = [(i, i + 1) for i in range(1, devices - 1, 2)]
    inner = [(i, i ^ 2) for i in range(devices)]
    outer = [(i, i + 2) for i in range(devices - 2) if i & 2]
    both = lambda pairs: pairs + [(j, i) for i, j in pairs]
    return dict(swap=swap, cross=both(cross), inner=inner, outer=both(outer))


def send_groups(device):
    core, chip = device % 2, (device // 2) % 2
    return dict(swap=2 - core, cross=1 + core, inner=3 - 3 * chip, outer=3 * chip)


def receive_groups(device):
    core, chip = device % 2, (device // 2) % 2
    return dict(swap=1 + core, cross=2 - core, inner=3 * chip, outer=3 - 3 * chip)


def exchange(sends):
    pairs = route_pairs(lax.axis_size("dom"))
    return {r: lax.ppermute(sends[r], "dom", pairs[r]) for r in ROUTES}


def pinned(value):
    return pltpu.with_memory_space_constraint(value, pltpu.VMEM)


def in_hbm(value):
    return pltpu.with_memory_space_constraint(value, pltpu.HBM)


def pick_kernel(part, halo, lam, *rest):
    outs, sems = dict(zip(ROUTES, rest[:4])), rest[4]
    groups = send_groups(lax.axis_index("dom"))
    copies = []
    for i, r in enumerate(ROUTES):
        for c in range(2):
            row = jnp.maximum(halo[0, c, groups[r]], 0)
            copies.append(
                pltpu.make_async_copy(lam.at[row, :, pl.ds(*part)], outs[r].at[c], sems.at[i, c])
            )
    for copy in copies:
        copy.start()
    for copy in copies:
        copy.wait()


def pick_sends(part, cost, place, halo, lam):
    sent = pltpu.VMEM((2, lam.shape[1], part[1]), lam.dtype)
    outs = pl.pallas_call(
        functools.partial(pick_kernel, part),
        name="pick_sends",
        out_shape=[sent] * 4,
        in_specs=[pl.BlockSpec(memory_space=pltpu.SMEM), pl.BlockSpec(memory_space=place)],
        out_specs=[pl.BlockSpec(memory_space=pltpu.VMEM)] * 4,
        scratch_shapes=[pltpu.SemaphoreType.DMA((4, 2))],
        compiler_params=pltpu.CompilerParams(vmem_limit_bytes=4 * 1024 * 1024),
        cost_estimate=pl.CostEstimate(flops=0, bytes_accessed=cost, transcendentals=0),
    )(in_hbm(halo), pltpu.with_memory_space_constraint(lam, place))
    return dict(zip(ROUTES, outs))


def lay_out_facts(facts, aux, gauges):
    wet, snapshots = facts[:2]
    owned, cells = wet.shape
    for i, fact in enumerate(facts[2:]):
        gauges[i : i + 1, :] = fact[...].astype(jnp.float32)
    for b in range(owned):
        rows = [wet[b : b + 1, :].astype(jnp.float32)]
        for t in range(snapshots.shape[0]):
            for c in range(3):
                rows.append(snapshots[t, b : b + 1, c * cells : (c + 1) * cells])
        rows.append(jnp.zeros((1, cells), jnp.float32))
        aux[b] = jnp.concatenate(rows, axis=0).T


def step_kernel(late, last, step, part, final, *refs):
    refs = list(refs)
    take = lambda n: [refs.pop(0) for _ in range(n)]
    cols, halo, lam, ops = take(4)
    begin = not late and step == 0
    facts = take(6) if begin else None
    aux, gauges = (None, None) if begin else take(2)
    received = take(4) if late else []
    take(1 + last if late else 0)
    done_squares = take(1)[0] if late and last else None
    base = take(1)[0] if late and last else None
    (new,) = take(1)
    raw, squares = take(2) if last else (None, None)
    base = take(1)[0] if last and not late else base
    sends = dict(zip(ROUTES, take(4))) if late and not last else {}
    if begin:
        aux, gauges, kept, kept_cols, kept_halo = take(5)
        ahead = [dict(zip(ROUTES, take(4))) for _ in range(PARTS - 1)]
        far, ops = ops, kept
    order = refs.pop(0)
    summed = refs.pop(0) if last else None
    (slots,) = refs if late else (None,)
    (op_sem,) = refs if begin else (None,)

    owned, entries = ops.shape[0], ops.shape[1]
    rows, width = lam.shape[1], part[1]
    cells = rows // 3
    here = pl.ds(*part)
    position = lax.axis_index("dom")

    def sent_rows():
        groups = send_groups(position)
        return [(r, c, jnp.maximum(halo[0, c, groups[r]], 0)) for r in ROUTES for c in range(2)]

    if late:
        groups = receive_groups(position)
        for i, r in enumerate(ROUTES):
            slots[pl.ds(2 * groups[r], 2)] = received[i][...]
    if last:
        summed[...] = jnp.zeros(summed.shape, jnp.float32)

    def fetch(b, p):
        pair = pl.ds(2 * p, 2)
        return pltpu.make_async_copy(far.at[b, pair], ops.at[b, pair], op_sem.at[b, p])

    def for_pairs(b, act):
        number = shape_of(b)[0]
        for p in range(entries // 2):

            @pl.when(number > p)
            def _(p=p):
                act(fetch(b, p))

    def shape_of(b):
        live, top = 0, -1
        for k in range(entries):
            live = live + (cols[b, k] >= 0).astype(jnp.int32)
            top = jnp.maximum(top, cols[b, k])
        return (live + 1) // 2, (top >= owned) if late else (top < owned)

    if begin:

        for own in (True, False):

            @pl.loop(0, owned)
            def _(b, own=own):
                @pl.when(shape_of(b)[1] == own)
                def _():
                    for_pairs(b, lambda copy: copy.start())

        lay_out_facts(facts, aux, gauges)
        for b in range(owned):
            for k in range(entries):
                kept_cols[b, k] = cols[b, k]
        for c in range(halo.shape[1]):
            for o in range(halo.shape[2]):
                kept_halo[0, c, o] = halo[0, c, o]
        for i, picks in enumerate(ahead):
            band = pl.ds((i + 1) * (part[1] // PARTS), part[1] // PARTS)
            for r, c, row in sent_rows():
                picks[r][c] = lam[row, :, band]

    first = gauges[1:2, here]
    active = jnp.where(
        jnp.logical_and(first <= step, step < first + gauges[2:3, here]), gauges[3:4, here], 0.0
    )
    own_cells = lax.broadcasted_iota(jnp.int32, (cells, width), 0)

    def prepare(b, total):
        base[b] = lam[b, :, here].astype(jnp.float32) + total
        raw[b, :, here] = from_snapshot(0, b, lambda c: lam[b, pl.ds(c * cells, cells), here])

    def from_snapshot(t, b, state, gathered=None):
        for c in range(3):
            column = 1 + 3 * t + c
            term = aux[b, :, column : column + 1] * state(c).astype(jnp.float32)
            gathered = term if gathered is None else gathered + term
        return gathered

    def finish(b, total, counted=None):
        wet = aux[b, :, 0:1]
        where = gauges[0:1, here].astype(jnp.int32) - (position * owned + b) * cells
        source = jnp.where(own_cells == where, active, 0.0)
        made = []
        for c in range(3):
            band = pl.ds(c * cells, cells)
            if base is not None and late:
                before = base[b, band, here]
            else:
                before = lam[b, band, here].astype(jnp.float32)
            updated = wet * (before + total[c * cells : (c + 1) * cells])
            if c == 0:
                updated = updated + source
            made.append(updated.astype(jnp.bfloat16))
            new[b, band, here] = made[c]
        if last:
            if late:
                gathered = raw[b, :, here]
            else:
                gathered = from_snapshot(0, b, lambda c: lam[b, pl.ds(c * cells, cells), here])
            gathered = from_snapshot(1, b, lambda c: made[c], gathered)
            raw[b, :, here] = gathered
            square = gathered * gathered
            if counted is not None:
                square = square * counted
            summed[...] += sum(square[i : i + 8] for i in range(0, cells, 8))

    def picked(b, k, local=True, received=late):
        col = cols[b, k]
        nothing = jnp.zeros((rows, width), lam.dtype)
        block = nothing
        if received:
            block = jnp.where(col >= owned, slots[jnp.maximum(col - owned, 0)], nothing)
        if local:
            own = lam[jnp.clip(col, 0, owned - 1), :, here]
            block = jnp.where(jnp.logical_and(col >= 0, col < owned), own, block)
        return block

    def row_total(b, entries_of, **kinds):
        state = [
            lam[b, :, here] if k == 0 and kinds.get("local", True) else picked(b, k, **kinds)
            for k in entries_of
        ]
        weights = jnp.concatenate([ops[b, k] for k in entries_of], axis=1)
        return jnp.dot(
            weights, jnp.concatenate(state, axis=0), preferred_element_type=jnp.float32
        )

    def by_twos():
        for n in range(1, entries // 2 + 1):
            count = 0
            for b in range(owned):
                pairs, mine = shape_of(b)
                order[n - 1, count] = b
                count = count + jnp.logical_and(mine, pairs == n).astype(jnp.int32)

            @pl.loop(0, (count + 1) // 2)
            def _(i, n=n, count=count):
                b, other = order[n - 1, 2 * i], order[n - 1, jnp.minimum(2 * i + 1, count - 1)]
                if begin:
                    for p in range(n):
                        fetch(b, p).wait()

                    @pl.when(other != b)
                    def _():
                        for p in range(n):
                            fetch(other, p).wait()

                total, ahead = (row_total(i, range(2 * n)) for i in (b, other))
                finish(b, total)
                finish(other, ahead, jnp.where(other != b, 1.0, 0.0))

    plain = True
    for b in range(owned):
        pairs, mine = shape_of(b)
        plain = jnp.logical_and(plain, jnp.logical_and(mine == late, pairs == 1))

    if late:
        @pl.when(plain)
        def _():
            taken = (1,) if last else (0, 1)
            split = dict(local=not last)
            total = row_total(0, taken, **split)
            for b in range(owned):
                ahead = row_total(b + 1, taken, **split) if b + 1 < owned else None
                finish(b, total)
                total = ahead

        @pl.when(jnp.logical_not(plain))
        def _():
            by_twos()
    else:
        by_twos()

    if last and not late:

        @pl.when(plain)
        def _():
            for b in range(owned):
                prepare(b, row_total(b, (0,)))

        @pl.when(jnp.logical_not(plain))
        def _():
            @pl.loop(0, owned)
            def _(b):
                @pl.when(jnp.logical_not(shape_of(b)[1]))
                def _():
                    prepare(b, 0.0)

    if last:
        sums = jnp.sum(summed[...], axis=0, keepdims=True)[None]
        if late:
            squares[...] = jnp.broadcast_to(done_squares[...], squares.shape)
            sums = sums + done_squares[:, :, here]
        squares[:, :, here] = jnp.broadcast_to(sums, (squares.shape[0], 1, width))

    if begin:

        @pl.loop(0, owned)
        def _(b):
            @pl.when(jnp.logical_not(shape_of(b)[1]))
            def _():
                for_pairs(b, lambda copy: copy.wait())

    if sends:
        for r, c, row in sent_rows():
            sends[r][c] = new[row, :, here]


def step_rows(
    late, last, step, part, final, cost, inputs, lam, received=None, before=None, base=None
):
    cols, halo, ops, facts = inputs
    owned, rows, width = lam.shape
    cells = rows // 3
    devices = lax.axis_size("dom")
    smem, vmem = (pl.BlockSpec(memory_space=m) for m in (pltpu.SMEM, pltpu.VMEM))
    begin = not late and step == 0
    args = [in_hbm(cols) if begin else cols, halo, pinned(lam), in_hbm(ops) if begin else pinned(ops), *facts]
    aliases = {}
    if late:
        args += [pinned(received[r]) for r in ROUTES]
        for i in range(1 + last):
            aliases[len(args)] = i
            args.append(pinned(before[i]))
        if last:
            args += [before[2], pinned(base)]
    out_shape = [pltpu.VMEM(lam.shape, lam.dtype)]
    if last:
        out_shape += [
            pltpu.VMEM((owned, cells, width), jnp.float32),
            pltpu.VMEM((devices if final else 1, 1, width), jnp.float32),
        ]
        if not late:
            out_shape.append(pltpu.VMEM(lam.shape, jnp.float32))
    elif late:
        out_shape += [pltpu.VMEM((2, rows, part[1]), lam.dtype)] * 4
    scratch = [pltpu.SMEM((ops.shape[1] // 2, owned), jnp.int32)]
    if last:
        scratch += [pltpu.VMEM((8, part[1]), jnp.float32)]
    if late:
        scratch += [pltpu.VMEM((owned, rows, part[1]), lam.dtype)]
    if begin:
        scratch += [pltpu.SemaphoreType.DMA((owned, ops.shape[1] // 2))]
        out_shape += [
            pltpu.VMEM((owned, cells, 2 + 3 * 2), jnp.float32),
            pltpu.VMEM((4, width), jnp.float32),
            pltpu.VMEM(ops.shape, ops.dtype),
            pltpu.SMEM(cols.shape, cols.dtype),
            pltpu.SMEM(halo.shape, halo.dtype),
        ] + [pltpu.VMEM((2, rows, width // PARTS), lam.dtype)] * (4 * (PARTS - 1))
    return pl.pallas_call(
        functools.partial(step_kernel, late, last, step, part, final),
        name=("late" if late else "early") + "_rows",
        out_shape=out_shape,
        in_specs=[smem, smem, vmem, pl.BlockSpec(memory_space=pltpu.HBM) if begin else vmem]
        + [vmem] * (len(args) - 4),
        out_specs=[smem if o.memory_space == pltpu.SMEM else vmem for o in out_shape],
        input_output_aliases=aliases,
        scratch_shapes=scratch,
        compiler_params=pltpu.CompilerParams(vmem_limit_bytes=16 * 1024 * 1024),
        cost_estimate=pl.CostEstimate(flops=0, bytes_accessed=cost, transcendentals=0),
    )(*args)


def scale_kernel(cells_total, sums, raw, out, scaled_rows, sems):
    factor = lax.rsqrt(jnp.sum(sums[...], axis=0) / cells_total + 1e-06)
    copies = []
    for b in range(raw.shape[0]):
        scaled_rows[b] = raw[b] * factor
        copies.append(pltpu.make_async_copy(scaled_rows.at[b], out.at[b], sems.at[b]))
        copies[b].start()
    for copy in copies:
        copy.wait()


def scaled(sums, raw, cells_total):
    vmem = pl.BlockSpec(memory_space=pltpu.VMEM)
    return pl.pallas_call(
        functools.partial(scale_kernel, cells_total),
        name="scale",
        out_shape=jax.ShapeDtypeStruct(raw.shape, raw.dtype),
        in_specs=[vmem, vmem],
        out_specs=pl.BlockSpec(memory_space=pltpu.HBM),
        scratch_shapes=[
            pltpu.VMEM(raw.shape, raw.dtype),
            pltpu.SemaphoreType.DMA((raw.shape[0],)),
        ],
        compiler_params=pltpu.CompilerParams(vmem_limit_bytes=8 * 1024 * 1024),
    )(sums, pinned(raw))


def per_device(
    adjoint_end,
    operator_blocks,
    block_cols,
    halo_send,
    wet_cells,
    gauge_cells,
    window_first,
    window_len,
    gauge_gain,
    snapshots,
):
    owned, cells = wet_cells.shape
    steps = snapshots.shape[0]
    devices = lax.axis_size("dom")
    halo = jnp.swapaxes(halo_send, 1, 2)
    facts = [wet_cells, in_hbm(snapshots)] + [
        v[None] for v in (gauge_cells, window_first, window_len, gauge_gain)
    ]
    width = adjoint_end.shape[2]
    parts = [(at, width // PARTS) for at in range(0, width, width // PARTS)]
    lam = adjoint_end
    received = [exchange(pick_sends(parts[0], PICK_COST, pltpu.HBM, halo, lam))]
    for step in range(steps):
        last = step == steps - 1
        inputs = (block_cols, halo, operator_blocks, facts)
        state = step_rows(False, last, step, (0, width), False, EARLY_COST, inputs, lam)
        base = None
        if last:
            *state, base = state
        if step == 0:
            state, (aux, gauges, *kept), picks = state[:1], state[1:6], state[6:]
            operator_blocks, block_cols, halo = kept
            received += [exchange(dict(zip(ROUTES, picks[i : i + 4]))) for i in range(0, len(picks), 4)]
            facts = [aux, gauges]
            inputs = (block_cols, halo, operator_blocks, facts)
        arriving, received = received, []
        for i, part in enumerate(parts):
            final = last and i == len(parts) - 1
            state = step_rows(
                True, last, step, part, final, LATE_COST[step][i], inputs, lam, arriving[i], state, base
            )
            if not last:
                received.append(exchange(dict(zip(ROUTES, state[1:]))))
        lam = state[0]
    raw, squares = state[1:]
    sums = lax.all_to_all(squares, "dom", 0, 0, tiled=True)
    return (lam, scaled(sums, raw, devices * owned * cells))


def solution(mesh):
    return jax.shard_map(
        per_device,
        mesh=mesh,
        in_specs=(
            P("dom", None, None),
            P("dom", None, None, None),
            P("dom", None),
            P("dom", None, None),
            P("dom", None),
            P(),
            P(),
            P(),
            P(),
            P(None, "dom", None),
        ),
        out_specs=(P("dom", None, None), P("dom", None, None)),
        check_vma=False,
    )
```
